32 devices in a mesh: dp: 2 (over x), seq: 16 (over z, y, core).
Axes of the slice: x: 2, y: 2, z: 4, core: 2. Of those that a mesh axis runs over, the one named last changes fastest.
Arguments:
- inputs: bfloat16 [4, 2048, 512], P('dp', 'seq'), may hold values from -6 to 6
- grad_out: bfloat16 [4, 2048, 512], P('dp', 'seq'), may hold values from -6 to 6
- seg_ids: int32 [4, 2048], P('dp', 'seq'), may hold values from 0 to 3, never falling along the last dimension, each value on 1 to 1024 neighbouring positions
- pad_mask: int32 [4, 2048], P('dp', 'seq'), may hold values 0 or 1
- w_query: bfloat16 [262144], P(('dp', 'seq')), may hold values from -1 to 1
- w_key: bfloat16 [262144], P(('dp', 'seq')), may hold values from -0.25 to 0.25
- w_value: bfloat16 [262144], P(('dp', 'seq')), may hold values from -0.25 to 0.25
- w_control: bfloat16 [262144], P(('dp', 'seq')), may hold values from -0.5 to 0.5
- w_out: bfloat16 [262144], P(('dp', 'seq')), may hold values from -0.75 to 0.75
- w_up: bfloat16 [1048576], P(('dp', 'seq')), may hold values from -0.25 to 0.25
- w_down: bfloat16 [1048576], P(('dp', 'seq')), may hold values from -0.125 to 0.125
- gain_attn: float32 [512], replicated, may hold values from 0.5 to 1.5
- gain_ffn: float32 [512], replicated, may hold values from 0.5 to 1.5
Outputs:
- output: bfloat16 [4, 2048, 512], P('dp', 'seq')
- grad_inputs: bfloat16 [4, 2048, 512], P('dp', 'seq')
- grad_query: float32 [262144], P(('dp', 'seq'))
- grad_key: float32 [262144], P(('dp', 'seq'))
- grad_value: float32 [262144], P(('dp', 'seq'))
- grad_control: float32 [262144], P(('dp', 'seq'))
- grad_outproj: float32 [262144], P(('dp', 'seq'))
- grad_up: float32 [1048576], P(('dp', 'seq'))
- grad_down: float32 [1048576], P(('dp', 'seq'))
- grad_gain_attn: float32 [512], replicated
- grad_gain_ffn: float32 [512], replicated
The draws below stay inside these ranges and needn't reach their ends.
Inputs may be any that keep to these rules, and one draw needn't show every extreme that they name: `seg_ids`: document ids start at 0 and never fall along a sequence; every id up to 3 is used; each document has 1 to 1024 tokens and one has exactly 1024.
All inputs are finite; a program needn't handle non-finite values. No bound on the sum of `pad_mask` on one device may be relied on, other than what follows from the above.
Results may differ from the reference program's by a relative error of at most 0.012.
The reference program's roundings to bfloat16 on the way count: a program that leaves them out, or rounds other values in their place, can miss the bound.
Values may be sent and summed in bfloat16 or wider, within the bound.
A program may use at most 128 MiB of HBM per device.

```python
import math
import jax
import jax.numpy as jnp
import numpy as np
from jax import lax

D = 512
H = 8
E = 64
S = 64
FF = 2048
CH = 128
DOCS = 4
HS = 512
L = 2048
SEQS = 4


def place_ends(values, key, least, high):
    extent = values.shape
    place = [jax.random.randint(jax.random.fold_in(key, axis), (), 0, extent[axis]) for axis in range(len(extent))]
    values = values.at[tuple(place)].set(least)
    longest = extent.index(max(extent))
    place[longest] = (place[longest] + 1) % extent[longest]
    return values.at[tuple(place)].set(high)


def levels(rng, dims, cuts, low, top_value):
    def one(position, shards_of):
        draws = jax.random.uniform(jax.random.fold_in(jax.random.fold_in(rng, 6), position), (shards_of,), jnp.float32, low / len(cuts), top_value / len(cuts))
        return jnp.repeat(jnp.exp(draws), dims[position] // shards_of).reshape((-1,) + (1,) * (len(dims) - position - 1))

    level = one(*cuts[0])
    for cut in cuts[1:]:
        level = level * one(*cut)
    return level


def split_up(count, total, bound, skew):
    portions = [(1 << 20) // math.isqrt(standing ** skew) + 1 for standing in range(2, count + 1)]
    rest, holding = total - bound - (count - 1), [1] * (count - 1)
    while rest > 0:
        candidates = [i for i in range(count - 1) if holding[i] < bound]
        whole, left = sum([portions[i] for i in candidates]), rest
        for i in candidates:
            addition = min(bound - holding[i], max(1, left * portions[i] // whole), rest)
            holding[i] = holding[i] + addition
            rest = rest - addition
    return np.array([bound] + holding)


def uneven(rng, amount, total, reach, lean):
    if amount == 2:
        one = jax.random.randint(rng, (), max(1, total - reach), min(reach, total - 1) + 1)
        return jnp.stack([one, total - one])
    lengths = jnp.asarray(split_up(amount, total, reach, lean), jnp.int32)
    couples = (amount - 1) // 2
    donor, taker = lengths[1:1 + 2 * couples:2], lengths[2:2 + 2 * couples:2]
    margin = jnp.minimum(donor - 1, reach - taker)
    shifted = jax.random.randint(jax.random.fold_in(rng, 1), (couples,), 0, 1 << 20) % (margin + 1)
    lengths = lengths.at[1:1 + 2 * couples:2].set(donor - shifted).at[2:2 + 2 * couples:2].set(taker + shifted)
    return lengths[jax.random.permutation(jax.random.fold_in(rng, 2), amount)]


def bell_draw(rng, extent, deviation, most, split=(), held_as=jnp.bfloat16):
    values = deviation * jax.random.normal(rng, extent, jnp.float32)
    if split:
        values = values * levels(rng, extent, split, -0.22, 0.18)
    return jnp.clip(values, -most, most).astype(held_as)


def setup_inputs(seed: int = 0) -> dict:
    seeds = jax.random.split(jax.random.key(seed), 14)
    return {
        "inputs": bell_draw(seeds[0], (SEQS, L, D), 1.0, 6.0, ((0, 2), (1, 16))),
        "grad_out": bell_draw(seeds[1], (SEQS, L, D), 1.0, 6.0, ((0, 2), (1, 16))),
        "seg_ids": jax.vmap(lambda own: jnp.searchsorted(jnp.cumsum(uneven(own, DOCS, L, L // 2, 1)), jnp.arange(L), side="right"))(jax.random.split(seeds[2], SEQS)).reshape((SEQS, L)).astype(jnp.int32),
        "pad_mask": place_ends((jax.random.randint(seeds[3], (SEQS, L), 0, 8) < 7).astype(jnp.int32), jax.random.fold_in(seeds[3], 1), 0, 1),
        "w_query": bell_draw(seeds[4], (D * D,), (D // 16) ** -0.5, 1.0, ((0, 32),)),
        "w_key": bell_draw(seeds[5], (D * D,), D ** -0.5, 0.25, ((0, 32),)),
        "w_value": bell_draw(seeds[6], (D * D,), D ** -0.5, 0.25, ((0, 32),)),
        "w_control": bell_draw(seeds[7], (D * HS,), (D // 4) ** -0.5, 0.5, ((0, 32),)),
        "w_out": bell_draw(seeds[8], (D * D,), (D // 8) ** -0.5, 0.75, ((0, 32),)),
        "w_up": bell_draw(seeds[9], (D * FF,), D ** -0.5, 0.25, ((0, 32),)),
        "w_down": bell_draw(seeds[10], (FF * D,), FF ** -0.5, 0.125, ((0, 32),)),
        "gain_attn": jnp.clip(1.0 + 0.1 * jax.random.normal(seeds[11], (D,), jnp.float32), 0.5, 1.5),
        "gain_ffn": jnp.clip(1.0 + 0.1 * jax.random.normal(seeds[12], (D,), jnp.float32), 0.5, 1.5),
    }


@jax.custom_vjp
def low(v):
    return lax.optimization_barrier(v.astype(jnp.bfloat16)).astype(jnp.float32)

@jax.custom_vjp
def low_back(v):
    return v

def low_keep(v):
    return (low(v), None)

def low_pass(kept, grad):
    return (grad,)

def back_keep(v):
    return (v, None)

def back_low(kept, grad):
    return (low(grad),)
low.defvjp(low_keep, low_pass)
low_back.defvjp(back_keep, back_low)
epsilon = 1e-05
highest = lax.Precision.HIGHEST

def layer_norm(values, gain):
    center = values - lax.optimization_barrier(jnp.mean(values, axis=-1, keepdims=True))
    spread = lax.optimization_barrier(jnp.mean(center * center, axis=-1, keepdims=True))
    return center * lax.rsqrt(spread + epsilon) * gain

def block_mix(q_rows, k_rows, v_rows, control, seg_rows, pad_rows, kv_in, z_in, seg_in):
    length_rows = seg_rows.shape[0]
    weight = jnp.exp(control) * pad_rows[:, None, None]
    places = jnp.arange(length_rows)
    same_doc = jnp.where((seg_rows[:, None] == seg_rows[None, :]) & (places[:, None] >= places[None, :]), 1.0, 0.0).astype(control.dtype)
    carry_use = jnp.where(seg_rows == seg_in, 1.0, 0.0).astype(control.dtype)[:, None, None]
    pair_dot = jnp.einsum('thd,ihd->hti', q_rows, k_rows, precision=highest) * same_doc[None]
    numerator = jnp.einsum('hti,ihs->ths', pair_dot, weight, precision=highest)
    numerator = numerator + carry_use * jnp.einsum('thd,hsd->ths', q_rows, kv_in[0], precision=highest)
    totals = jnp.einsum('ti,ihs->ths', same_doc, weight, precision=highest) + carry_use * z_in[None]
    floors = jnp.maximum(totals, 1.0)
    scores = numerator / (floors * math.sqrt(q_rows.shape[-1]))
    slot_prob = jax.nn.softmax(scores, axis=-1)
    shares = slot_prob / floors
    mixing = jnp.einsum('ths,ihs->hti', shares, weight, precision=highest) * same_doc[None]
    result = jnp.einsum('hti,ihd->thd', mixing, v_rows, precision=highest)
    return result + carry_use * jnp.einsum('ths,hsd->thd', shares, kv_in[1], precision=highest)

def block_summary(k_rows, v_rows, control, seg_rows, pad_rows):
    last_doc = jnp.where(seg_rows == seg_rows[-1], 1.0, 0.0).astype(control.dtype)
    weight = jnp.exp(control) * (pad_rows * last_doc)[:, None, None]
    key_sum = jnp.einsum('ths,thd->hsd', weight, k_rows, precision=highest)
    value_sum = jnp.einsum('ths,thd->hsd', weight, v_rows, precision=highest)
    return (jnp.stack([key_sum, value_sum]), lax.optimization_barrier(jnp.sum(weight, axis=0)))

def sequence_forward(x_seq, seg_seq, pad_seq, matrices, gain_attn, gain_ffn):
    w_query, w_key, w_value, w_control, w_out, w_up, w_down = matrices
    length_seq = x_seq.shape[0]
    blocks = length_seq // CH
    norm_one = low(layer_norm(x_seq, gain_attn))
    q_all = low_back(low(jnp.dot(norm_one, w_query, precision=highest)))
    k_all = low_back(low(jnp.dot(norm_one, w_key, precision=highest)))
    v_all = low_back(low(jnp.dot(norm_one, w_value, precision=highest)))
    c_all = low_back(jnp.dot(norm_one, w_control, precision=highest))
    pieces = (q_all.reshape(blocks, CH, H, E), k_all.reshape(blocks, CH, H, E), v_all.reshape(blocks, CH, H, E), c_all.reshape(blocks, CH, H, S), seg_seq.reshape(blocks, CH), pad_seq.reshape(blocks, CH))

    def advance(state, block_in):
        q_rows, k_rows, v_rows, c_rows, seg_rows, pad_rows = block_in
        kv_in, z_in, seg_in = state
        mixed_block = block_mix(q_rows, k_rows, v_rows, c_rows, seg_rows, pad_rows, kv_in, z_in, seg_in)
        kv_loc, z_loc = block_summary(k_rows, v_rows, c_rows, seg_rows, pad_rows)
        keep = jnp.where(seg_in == seg_rows[-1], 1.0, 0.0).astype(z_in.dtype)
        return ((kv_loc + keep * kv_in, z_loc + keep * z_in, seg_rows[-1]), mixed_block)
    start = (jnp.zeros((2, H, S, E), jnp.float32), jnp.zeros((H, S), jnp.float32), jnp.full((), -1.0, jnp.float32))
    _, mixed_all = lax.scan(jax.checkpoint(advance), start, pieces)
    mixed_rows = low(mixed_all.reshape(length_seq, D))
    attn = low_back(jnp.dot(mixed_rows, w_out, precision=highest))
    residual = x_seq + attn
    norm_two = low(layer_norm(residual, gain_ffn))
    hidden = low(jax.nn.silu(low_back(jnp.dot(norm_two, w_up, precision=highest))))
    return residual + jnp.dot(hidden, w_down, precision=highest)

def reference(inputs, grad_out, seg_ids, pad_mask, w_query, w_key, w_value, w_control, w_out, w_up, w_down, gain_attn, gain_ffn):
    shapes = ((D, D), (D, D), (D, D), (D, HS), (D, D), (D, FF), (FF, D))
    flats = (w_query, w_key, w_value, w_control, w_out, w_up, w_down)
    matrices = tuple((flat_w.astype(jnp.float32).reshape(form_of) for flat_w, form_of in zip(flats, shapes)))
    seg_float = seg_ids.astype(jnp.float32)
    pad_float = pad_mask.astype(jnp.float32)

    def forward(mats_in, gain_a, gain_f, x_all):

        def one_sequence(slices):
            return sequence_forward(slices[0], slices[1], slices[2], mats_in, gain_a, gain_f)
        return lax.map(jax.checkpoint(one_sequence), (x_all, seg_float, pad_float))
    result, pull_back = jax.vjp(forward, matrices, gain_attn.astype(jnp.float32), gain_ffn.astype(jnp.float32), inputs.astype(jnp.float32))
    grad_mats, grad_a, grad_f, grad_x = pull_back(grad_out.astype(jnp.float32))
    return (result.astype(jnp.bfloat16), grad_x.astype(jnp.bfloat16), grad_mats[0].reshape(-1), grad_mats[1].reshape(-1), grad_mats[2].reshape(-1), grad_mats[3].reshape(-1), grad_mats[4].reshape(-1), grad_mats[5].reshape(-1), grad_mats[6].reshape(-1), grad_a, grad_f)
```

```python
import functools

import jax
import jax.numpy as jnp
from jax import lax
from jax.experimental import pallas as pl
from jax.experimental.pallas import tpu as pltpu
from jax.sharding import PartitionSpec as P

D = 512
FF = 2048
TOK = 128
SEQB = 2
OUTER = 4
BF = jnp.bfloat16
F32 = jnp.float32
EPS = 1e-05
MESH = pl.DeviceIdType.MESH
AXES = "aoic"


def nn(a, b):
    return jnp.dot(a, b, preferred_element_type=F32)


def nt(a, b):
    return lax.dot_general(a, b, (((1,), (1,)), ((), ())), preferred_element_type=F32)


def tn(a, b):
    return lax.dot_general(a, b, (((0,), (0,)), ((), ())), preferred_element_type=F32)


def halves(v):
    high = v.astype(BF)
    return high, (v - high.astype(F32)).astype(BF)


def norm_rows(v):
    center = v - jnp.mean(v, axis=-1, keepdims=True)
    inv = lax.rsqrt(jnp.mean(center * center, axis=-1, keepdims=True) + EPS)
    return center * inv, inv


def norm_back(g, unit, inv):
    return inv * (
        g - jnp.mean(g, axis=-1, keepdims=True) - unit * jnp.mean(g * unit, axis=-1, keepdims=True)
    )


def layout(na, ni):
    nch = OUTER * ni
    rows = 512 // nch
    lead = (na, OUTER, ni, 2)
    s = {}

    def vm(name, shape, dtype):
        s[name] = pltpu.VMEM(tuple(shape), dtype)

    vm("tmp", (256, 128), F32)
    vm("agq", lead + (16, 1024), BF)
    vm("sendq", (16, 1024), BF)
    vm("ago", lead + (16, 512), BF)
    vm("agu", lead + (16, FF), BF)
    vm("agd", lead + (64, 512), BF)
    vm("unit1", (256, 512), F32)
    vm("inv1", (256, 128), F32)
    vm("norm1", (SEQB, 2, TOK, 512), BF)
    vm("mini", (2, 8, 128), F32)
    for m in ("mask", "maskt"):
        vm(m, (SEQB, 256, 256), F32)
    for m in ("last", "use", "padb"):
        vm(m, (SEQB, 256, 128), F32)
    for m in ("q", "k", "v", "whi", "wlo"):
        vm(m, (4, 256, 128), BF)
    for m in ("w", "num", "tot", "share", "score", "dtot", "dkl", "dvl", "dwl"):
        vm(m, (4, 256, 128), F32)
    vm("dnum", (4, 256, 128), BF)
    vm("info", (8, 128), F32)
    for m in ("sloc", "rcv", "dloc", "drcv"):
        vm(m, (nch, rows + 8, 128), F32)
    for m in ("snd", "stin", "dsnd", "gin"):
        vm(m, (nch, rows, 128), F32)
    vm("zin", (8, 128), F32)
    vm("gz", (8, 128), F32)
    vm("outb", (4, 2, TOK, 128), BF)
    vm("mixx", (2, 4, TOK, 128), BF)
    vm("mixed", (256, 512), BF)
    for m in ("res", "unit2", "yacc", "dn2", "dres"):
        vm(m, (256, 512), F32)
    vm("inv2", (256, 128), F32)
    vm("n2", (256, 512), BF)
    vm("do", (4, 2, TOK, 128), BF)
    vm("senddo", (4, TOK, 128), BF)
    vm("dd", (SEQB, 2, TOK, 1024), BF)
    vm("dn1", (2, SEQB, TOK, 512), F32)
    vm("dn1r", (SEQB, TOK, 512), F32)
    vm("gq", lead + (16, 1024), BF)
    vm("go", lead + (16, 512), BF)
    vm("gu", lead + (16, FF), BF)
    vm("gd", lead + (64, 512), BF)
    vm("final", (2, 16, 1024), F32)
    vm("fsend", (16, 1024), F32)
    for ax, size in (("c", 2), ("i", ni), ("a", na), ("o", OUTER)):
        vm("gain_" + ax, (size, 8, 512), F32)
    for name, _, order, width, height in pieces(na, ni):
        dims = list(AXES)
        for step, ax in enumerate(order):
            size = dict(a=na, o=OUTER, i=ni, c=2)
            dims.remove(ax)
            left = tuple(size[d] for d in dims)
            vm(f"r{name}{step}", (max(size[ax] - 1, 1),) + left + (height, width), BF)
            if step < len(order) - 1:
                vm(f"s{name}{step}", left + (height, width), BF)
    s["sems"] = pltpu.SemaphoreType.DMA((2 * 200,))
    return s


def pieces(na, ni):
    return (
        ("q", "gq", "iao", 256, 16),
        ("k", "gq", "aio", 256, 16),
        ("v", "gq", "iao", 256, 16),
        ("x", "gq", "aio", 256, 16),
        ("o", "go", "ciao", 512, 16),
        ("u0", "gu", "ciao", 1024, 16),
        ("u1", "gu", "caio", 1024, 16),
        ("d0", "gd", "ciao", 256, 64),
        ("d1", "gd", "caio", 256, 64),
    )


def kernel(na, ni, names, *refs):
    (x_ref, dy_ref, seg_ref, pad_ref, wq_ref, wk_ref, wv_ref, wc_ref, wo_ref, wu_ref, wd_ref) = refs[:11]
    ga_ref, gf_ref = refs[11:13]
    (y_ref, dx_ref, oq_ref, ok_ref, ov_ref, oc_ref, oo_ref, ou_ref, od_ref, og1_ref, og2_ref) = refs[13:24]
    r = dict(zip(names, refs[24:], strict=True))
    nch = OUTER * ni
    rows = 512 // nch
    per = 64 // rows

    dp = lax.axis_index("dp")
    seq = lax.axis_index("seq")
    chip = seq // 2
    at = dict(a=dp if na > 1 else 0, o=chip // ni, i=lax.rem(chip, ni), c=lax.rem(seq, 2))
    size = dict(a=na, o=OUTER, i=ni, c=2)
    core = at["c"]

    def device(**moved):
        p = {**at, **moved}
        return (p["a"] if na > 1 else dp, (p["o"] * ni + p["i"]) * 2 + p["c"])

    def chip_device(t):
        return (dp, t * 2 + core)

    started = []
    sems = r["sems"]

    def remote(src, dst, dev):
        n = len(started)
        copy = pltpu.make_async_remote_copy(
            src_ref=src,
            dst_ref=dst,
            send_sem=sems.at[2 * n],
            recv_sem=sems.at[2 * n + 1],
            device_id=dev,
            device_id_type=MESH,
        )
        copy.start()
        started.append(copy)
        return copy

    def arrived(copies):
        for copy in copies:
            copy.wait_recv()

    mate = device(c=1 - core)

    barrier = pltpu.get_barrier_semaphore()
    greet = [mate] + [chip_device(lax.rem(chip + k, nch)) for k in range(1, nch)]
    greet += [device(a=lax.rem(at["a"] + k, na)) for k in range(1, na)]
    for dev in greet:
        pl.semaphore_signal(barrier, inc=1, device_id=dev, device_id_type=MESH)

    lane = lax.broadcasted_iota(jnp.int32, (1, 128), 1)
    low = (lane < 64).astype(F32)
    high = 1.0 - low
    lowb, highb = low.astype(BF), high.astype(BF)
    hm = (lowb, highb)
    first_core = core == 0

    tmp = r["tmp"]

    def unpack(ref, height, width):
        lines = height * width // 128
        tmp[0:lines, :] = ref[...].astype(F32)
        step = width // 128
        return [tmp[pl.ds(j, height, stride=step), :].astype(BF) for j in range(step)]

    own = (at["a"], at["o"], at["i"], core)
    agq, ago, agu, agd = r["agq"], r["ago"], r["agu"], r["agd"]
    for w, ref in enumerate((wq_ref, wk_ref, wv_ref, wc_ref)):
        blk = unpack(ref, 16, 512)
        for j in range(2):
            cols = slice(w * 256 + j * 128, w * 256 + j * 128 + 128)
            agq[own + (slice(None), cols)] = jnp.where(first_core, blk[j], blk[2 + j])
            r["sendq"][:, cols] = jnp.where(first_core, blk[2 + j], blk[j])
    for ref, buf, height, width in ((wo_ref, ago, 16, 512), (wu_ref, agu, 16, FF), (wd_ref, agd, 64, 512)):
        for j, blk in enumerate(unpack(ref, height, width)):
            buf[own + (slice(None), slice(j * 128, j * 128 + 128))] = blk

    x = x_ref[...].reshape(256, 512).astype(F32)
    unit, inv = norm_rows(x)
    r["unit1"][...] = unit
    r["inv1"][...] = jnp.broadcast_to(inv, (256, 128))
    n1own = (unit * ga_ref[...]).astype(BF)
    norm1 = r["norm1"]
    for b in range(SEQB):
        norm1[b, core] = n1own[b * TOK : (b + 1) * TOK]
    mini = r["mini"]
    mini[core, 0:2, :] = seg_ref[...].astype(F32)
    mini[core, 2:4, :] = pad_ref[...].astype(F32)
    mini[core, 4:8, :] = jnp.zeros((4, 128), F32)

    pl.semaphore_wait(barrier, len(greet))

    swap_w = remote(r["sendq"], agq.at[own], mate)
    swap_m = remote(mini.at[core], mini.at[core], mate)
    swap_n = remote(norm1.at[:, core], norm1.at[:, core], mate)

    def gather(buf, axis, done, lo, width):
        cols = pl.ds(lo, width)
        index = tuple(slice(None) if d in done else pl.ds(at[d], 1) for d in AXES)
        ref = buf.at[index + (slice(None), cols)]
        return [
            remote(ref, ref, device(**{axis: lax.rem(at[axis] + k, size[axis])}))
            for k in range(1, size[axis])
        ]

    swap_w.wait_recv()
    first = ((768, "ia"), (256, "ai"), (512, "ia"), (0, "ai"))
    rest = (
        (ago, 0, 512, "ia"),
        (agu, 0, 1024, "ai"),
        (agu, 1024, 1024, "ia"),
        (agd, 0, 256, "ai"),
        (agd, 256, 256, "ia"),
    )
    step_o = [gather(agq, "o", "c", lo, 256) for lo, _ in first]
    step_1, step_2 = [], []
    for (lo, order), got in zip(first, step_o):
        arrived(got)
        step_1.append(gather(agq, order[0], "co", lo, 256))
    rest_o = [gather(buf, "o", "", lo, width) for buf, lo, width, _ in rest]

    arrived([swap_m, swap_n])
    turned = [mini[s].T for s in range(2)]
    big_row = lax.broadcasted_iota(jnp.int32, (256, 256), 0)
    big_col = lax.broadcasted_iota(jnp.int32, (256, 256), 1)
    for b in range(SEQB):
        seg_row = jnp.concatenate([mini[0, b : b + 1, :], mini[1, b : b + 1, :]], axis=1)
        seg_col = jnp.concatenate([t[:, b : b + 1] for t in turned], axis=0)
        pad_col = jnp.concatenate([t[:, 2 + b : 3 + b] for t in turned], axis=0)
        same = seg_col == seg_row
        r["mask"][b] = jnp.where(same & (big_row >= big_col), 1.0, 0.0)
        r["maskt"][b] = jnp.where(same & (big_row <= big_col), 1.0, 0.0)
        seg_last = seg_row[:, 255:256]
        r["last"][b] = jnp.broadcast_to((seg_col == seg_last).astype(F32), (256, 128))
        r["padb"][b] = jnp.broadcast_to(pad_col, (256, 128))
        r["info"][4 + b : 5 + b, :] = jnp.broadcast_to(seg_last, (1, 128))
        r["info"][6 + b : 7 + b, :] = jnp.broadcast_to(seg_row[:, 0:1], (1, 128))

    for (lo, order), got in zip(first, step_1):
        arrived(got)
        step_2.append(gather(agq, order[1], "co" + order[0], lo, 256))

    def project(w):
        arrived(step_2[{3: 0, 1: 1, 2: 2, 0: 3}[w]])
        mat = agq[..., w * 256 : w * 256 + 256].reshape(512, 256)
        for b in range(SEQB):
            out = nn(norm1[b].reshape(256, 512), mat)
            for pair in range(2):
                part = out[:, pair * 128 : pair * 128 + 128]
                n = b * 2 + pair
                if w == 3:
                    weight = jnp.exp(part) * r["padb"][b]
                    r["w"][n] = weight
                    r["whi"][n], r["wlo"][n] = halves(weight)
                else:
                    r[("q", "k", "v")[w]][n] = part.astype(BF)

    for w in (3, 1, 2):
        project(w)

    def fold(full):
        return full[0:64] * low + full[64:128] * high

    def put_state(ref, n, which, value):
        for t in range(per):
            ref[(n * 2 + which) * per + t, 0:rows, :] = value[t * rows : (t + 1) * rows]

    def get_block(ref, n, which):
        value = ref[pl.ds((n * 2 + which) * per, per)].reshape(64, 128)
        return jnp.concatenate([value * low, value * high], axis=0)

    def local_state(n, carry):
        weight = r["w"][n] * r["last"][n // 2]
        hi, lo = halves(weight)
        for which, name in ((0, "k"), (1, "v")):
            rhs = r[name][n]
            put_state(r["sloc"], n, which, fold(tn(hi, rhs) + tn(lo, rhs)))
        r["info"][pl.ds(n, 1), :] = jnp.sum(weight, axis=0, keepdims=True)
        return carry

    lax.fori_loop(0, 4, local_state, 0)

    def spread(src, dst, info):
        for t in range(nch):
            src[t, rows : rows + 8, :] = info
        dst[chip] = src[chip]
        return [
            remote(src.at[lax.rem(chip + k, nch)], dst.at[chip], chip_device(lax.rem(chip + k, nch)))
            for k in range(1, nch)
        ]

    def back(src, dst):
        dst[chip] = src[chip]
        return [
            remote(src.at[lax.rem(chip + k, nch)], dst.at[chip], chip_device(lax.rem(chip + k, nch)))
            for k in range(1, nch)
        ]

    out_1 = spread(r["sloc"], r["rcv"], r["info"][...])

    project(0)
    rest_1 = []
    for (buf, lo, width, order), got in zip(rest, rest_o):
        arrived(got)
        rest_1.append(gather(buf, order[0], "o", lo, width))

    def mix_local(n, carry):
        q, k, whi, wlo = r["q"][n], r["k"][n], r["whi"][n], r["wlo"][n]
        mask = r["mask"][n // 2]
        num = jnp.zeros((256, 128), F32)
        for m in hm:
            hi, lo = halves(nt(q * m, k) * mask)
            num += nn(hi, whi * m) + nn(lo, whi * m) + nn(hi, wlo * m)
        r["num"][n] = num
        maskb = mask.astype(BF)
        r["tot"][n] = nn(maskb, whi) + nn(maskb, wlo)
        return carry

    lax.fori_loop(0, 4, mix_local, 0)

    arrived(out_1)
    rcv = r["rcv"]
    owned = (chip * rows) // 256

    def last_of(p, b):
        return rcv[p, pl.ds(rows + 4 + b, 1), :]

    def first_of(p, b):
        return rcv[p, pl.ds(rows + 6 + b, 1), :]

    run = jnp.zeros((rows, 128), F32)
    for p in range(nch):
        r["snd"][p] = run
        if p == 0:
            run = rcv[0, 0:rows, :]
        else:
            keep = (last_of(p - 1, owned) == last_of(p, owned)).astype(F32)
            run = rcv[p, 0:rows, :] + keep * run
    out_2 = back(r["snd"], r["stin"])
    zrun = [jnp.zeros((2, 128), F32) for _ in range(SEQB)]
    for p in range(nch - 1):
        for b in range(SEQB):
            z = rcv[p, rows + 2 * b : rows + 2 * b + 2, :]
            if p > 0:
                z = z + (last_of(p - 1, b) == last_of(p, b)).astype(F32) * zrun[b]
            zrun[b] = jnp.where(p < chip, z, zrun[b])
    before = jnp.maximum(chip - 1, 0)
    for b in range(SEQB):
        r["zin"][2 * b : 2 * b + 2, :] = zrun[b]
        open_doc = jnp.where(chip > 0, last_of(before, b), -1.0)[:, 0:1]
        seg_col = jnp.concatenate([t[:, b : b + 1] for t in turned], axis=0)
        r["use"][b] = jnp.broadcast_to((seg_col == open_doc).astype(F32), (256, 128))

    rest_2 = []
    for (buf, lo, width, order), got in zip(rest, rest_1):
        arrived(got)
        rest_2.append(gather(buf, order[1], "o" + order[0], lo, width))

    arrived(out_2)

    def both(op, v):
        if op is jnp.max:
            a = jnp.max(jnp.where(lane < 64, v, -jnp.inf), axis=1, keepdims=True)
            b = jnp.max(jnp.where(lane < 64, -jnp.inf, v), axis=1, keepdims=True)
        else:
            a = jnp.sum(v * low, axis=1, keepdims=True)
            b = jnp.sum(v * high, axis=1, keepdims=True)
        return jnp.where(lane < 64, a, b)

    def mix_rest(n, carry):
        b = n // 2
        q, v, whi = r["q"][n], r["v"][n], r["whi"][n]
        mask, use = r["mask"][b], r["use"][b]
        khi, klo = halves(get_block(r["stin"], n, 0))
        num = r["num"][n] + use * (nt(q, khi) + nt(q, klo))
        tot = r["tot"][n] + use * r["zin"][pl.ds(n, 1), :]
        floor = jnp.maximum(tot, 1.0)
        score = num / (floor * 8.0)
        e = jnp.exp(score - both(jnp.max, score))
        share = e / (both(jnp.sum, e) * floor)
        r["tot"][n] = tot
        r["score"][n] = score
        r["share"][n] = share
        sb = share.astype(BF)
        out = use * nn(sb, get_block(r["stin"], n, 1).astype(BF))
        for m in hm:
            out += nn((nt(sb * m, whi) * mask).astype(BF), v * m)
        r["outb"][n] = out.astype(BF).reshape(2, TOK, 128)
        return carry

    lax.fori_loop(0, 4, mix_rest, 0)
    swap_o = remote(r["outb"].at[:, 1 - core], r["mixx"].at[core], mate)
    for n in range(4):
        r["mixx"][core, n] = r["outb"][n, core]

    rest_3 = []
    for (buf, lo, width, order), got in zip(rest, rest_2):
        arrived(got)
        rest_3.append(gather(buf, "c", "oai", lo, width))

    swap_o.wait_recv()
    arrived(rest_3[0])
    mixx = r["mixx"]
    for b in range(SEQB):
        r["mixed"][b * TOK : (b + 1) * TOK, :] = jnp.concatenate(
            [mixx[h, b * 2 + p] for h in range(2) for p in range(2)], axis=1
        )
    w_out = ago[...].reshape(512, 512)
    residual = x_ref[...].reshape(256, 512).astype(F32) + nn(r["mixed"][...], w_out)
    r["res"][...] = residual
    unit, inv = norm_rows(residual)
    r["unit2"][...] = unit
    r["inv2"][...] = jnp.broadcast_to(inv, (256, 128))
    r["n2"][...] = (unit * gf_ref[...]).astype(BF)
    for copies in rest_3[1:]:
        arrived(copies)

    r["yacc"][...] = jnp.zeros((256, 512), F32)
    r["dn2"][...] = jnp.zeros((256, 512), F32)
    span = na * OUTER // 4

    def feed(j, carry):
        dy = dy_ref[...].reshape(256, 512)
        n2 = r["n2"][...]
        cols = pl.ds(pl.multiple_of(j * 512, 512), 512)
        up = agu[:, :, :, :, :, cols].reshape(512, 512)
        place = (j * span // OUTER, pl.ds(lax.rem(j * span, OUTER), span))
        down = agd[place].reshape(512, 512)
        pre = nn(n2, up)
        sig = 1.0 / (1.0 + jnp.exp(-pre))
        hidden = (pre * sig).astype(BF)
        r["yacc"][...] += nn(hidden, down)
        d_pre = (nt(dy, down) * (sig * (1.0 + pre * (1.0 - sig)))).astype(BF)
        r["dn2"][...] += nt(d_pre, up)
        r["gd"][place] = tn(hidden, dy).astype(BF).reshape((span, ni, 2, 64, 512))
        r["gu"][:, :, :, :, :, cols] = tn(n2, d_pre).astype(BF).reshape((na, OUTER, ni, 2, 16, 512))
        return carry

    lax.fori_loop(0, 4, feed, 0)

    class Sum:
        def __init__(self, name, buffer, order, width, height, lo):
            self.name, self.order, self.width, self.height = name, order, width, height
            self.ref, self.lo, self.dims, self.step = r[buffer], lo, list(AXES), 0

        def start(self):
            ax = self.order[self.step]
            p = self.dims.index(ax)
            cols = pl.ds(self.lo, self.width)
            land = r[f"r{self.name}{self.step}"]
            self.copies = []
            for k in range(1, size[ax]):
                to = lax.rem(at[ax] + k, size[ax])
                index = [slice(None)] * len(self.dims) + [slice(None), cols]
                index[p] = to
                self.copies.append(remote(self.ref.at[tuple(index)], land.at[k - 1], device(**{ax: to})))

        def finish(self, emit=None):
            ax = self.order[self.step]
            p = self.dims.index(ax)
            arrived(self.copies)
            land = r[f"r{self.name}{self.step}"]
            cols = slice(self.lo, self.lo + self.width)
            left = [size[d] for d in self.dims if d != ax]
            total = 1
            for extent in left:
                total *= extent
            into = None if emit else r[f"s{self.name}{self.step}"]

            def one(flat):
                index, rest_of = [], flat
                for extent in reversed(left):
                    index.insert(0, rest_of % extent if isinstance(rest_of, int) else lax.rem(rest_of, extent))
                    rest_of = rest_of // extent
                full = list(index)
                full.insert(p, at[ax])
                value = self.ref[tuple(full) + (slice(None), cols)].astype(F32)
                for k in range(size[ax] - 1):
                    value += land[(k,) + tuple(index)].astype(F32)
                if emit:
                    emit(index, value)
                else:
                    into[tuple(index)] = value.astype(BF)

            if total <= 2:
                for flat in range(total):
                    one(flat)
            else:
                def body(flat, carry):
                    one(flat)
                    return carry

                lax.fori_loop(0, total, body, 0)
            self.dims.remove(ax)
            self.ref, self.lo, self.step = into, 0, self.step + 1

    specs = {name: (name, buf, order, width, height) for name, buf, order, width, height in pieces(na, ni)}
    place = dict(q=0, k=256, v=512, x=768, o=0, u0=0, u1=1024, d0=0, d1=256)
    sums = {name: Sum(*spec, place[name]) for name, spec in specs.items()}
    ffn = [sums[n] for n in ("d0", "d1", "u0", "u1")]
    for s in ffn:
        s.start()

    y_ref[...] = (r["res"][...] + r["yacc"][...]).astype(BF).reshape(SEQB, TOK, 512)
    dn2 = r["dn2"][...]
    unit = r["unit2"][...]
    gains2 = jnp.sum(dn2 * unit, axis=0, keepdims=True)
    d_res = dy_ref[...].reshape(256, 512).astype(F32) + norm_back(
        dn2 * gf_ref[...], unit, r["inv2"][:, 0:1]
    )
    r["dres"][...] = d_res
    d_attn = d_res.astype(BF)
    d_mixed = nt(d_attn, w_out).astype(BF)
    for b in range(SEQB):
        for p in range(2):
            part = [d_mixed[b * TOK : (b + 1) * TOK, h * 256 + p * 128 : h * 256 + p * 128 + 128] for h in range(2)]
            r["do"][b * 2 + p, core] = jnp.where(first_core, part[0], part[1])
            r["senddo"][b * 2 + p] = jnp.where(first_core, part[1], part[0])
    swap_d = remote(r["senddo"], r["do"].at[:, core], mate)
    r["go"][...] = tn(r["mixed"][...], d_attn).astype(BF).reshape((na, OUTER, ni, 2, 16, 512))
    sums["o"].start()
    for s in ffn:
        s.finish()
        s.start()
    sums["o"].finish()
    sums["o"].start()
    swap_d.wait_recv()

    def mix_back(n, carry):
        b = n // 2
        q, v, whi = r["q"][n], r["v"][n], r["whi"][n]
        mask, use = r["mask"][b], r["use"][b]
        share, tot, score = r["share"][n], r["tot"][n], r["score"][n]
        d_out = r["do"][n].reshape(256, 128)
        ds = use * nt(d_out, get_block(r["stin"], n, 1).astype(BF))
        for m in hm:
            ds += nn((nt(d_out * m, v) * mask).astype(BF), whi * m)
        floor = jnp.maximum(tot, 1.0)
        inv_floor = 1.0 / floor
        prob = share * floor
        dprob = ds * inv_floor
        dscore = prob * (dprob - both(jnp.sum, dprob * prob))
        dnum = dscore * inv_floor * 0.125
        gate = jnp.where(tot > 1.0, 1.0, jnp.where(tot == 1.0, 0.5, 0.0))
        dtot = -(ds * share + dscore * score) * inv_floor * gate
        r["dnum"][n] = dnum.astype(BF)
        r["dtot"][n] = dtot
        put_state(r["dloc"], n, 0, fold(tn((use * dnum).astype(BF), q)))
        put_state(r["dloc"], n, 1, fold(tn((use * share).astype(BF), d_out)))
        r["gz"][pl.ds(n, 1), :] = jnp.sum(use * dtot, axis=0, keepdims=True)
        return carry

    lax.fori_loop(0, 4, mix_back, 0)
    r["gz"][4:8, :] = jnp.zeros((4, 128), F32)
    out_3 = spread(r["dloc"], r["drcv"], r["gz"][...])

    def mix_back_local(n, carry):
        b = n // 2
        q, k, v, whi, w = r["q"][n], r["k"][n], r["v"][n], r["whi"][n], r["w"][n]
        mask, maskt, use = r["mask"][b], r["maskt"][b], r["use"][b]
        d_out, dnum = r["do"][n].reshape(256, 128), r["dnum"][n]
        sb = r["share"][n].astype(BF)
        dq = use * nn(dnum, get_block(r["stin"], n, 0).astype(BF))
        dk = jnp.zeros((256, 128), F32)
        dv = jnp.zeros((256, 128), F32)
        dw = nn(maskt.astype(BF), r["dtot"][n].astype(BF))
        for m in hm:
            dq += nn((nt(dnum * m, whi) * mask).astype(BF), k * m)
            dk += nn((nt(whi * m, dnum) * maskt).astype(BF), q * m)
            dv += nn((nt(whi * m, sb) * maskt).astype(BF), d_out * m)
            dw += nn((nt(v * m, d_out) * maskt).astype(BF), sb * m)
            dw += nn((nt(k * m, q) * maskt).astype(BF), dnum * m)
        cols = pl.ds(pl.multiple_of(lax.rem(n, 2) * 128, 128), 128)
        r["dd"][b, :, :, cols] = dq.astype(BF).reshape(2, TOK, 128)
        r["dkl"][n] = dk
        r["dvl"][n] = dv
        r["dwl"][n] = dw
        return carry

    lax.fori_loop(0, 4, mix_back_local, 0)
    dd = r["dd"]

    def weight_gradient(lo, width):
        left = norm1[...].reshape(512, 512)
        value = tn(left, dd[:, :, :, lo : lo + width].reshape(512, width))
        r["gq"][:, :, :, :, :, lo : lo + width] = value.astype(BF).reshape((na, OUTER, ni, 2, 16, width))

    weight_gradient(0, 256)
    sums["q"].start()
    for s in ffn:
        s.finish()
        s.start()
    sums["o"].finish()
    sums["o"].start()

    arrived(out_3)
    drcv = r["drcv"]
    run = jnp.zeros((rows, 128), F32)
    for p in reversed(range(nch)):
        r["dsnd"][p] = run
        if p == nch - 1:
            run = drcv[p, 0:rows, :]
        else:
            keep = (first_of(p, owned) == first_of(p + 1, owned)).astype(F32)
            run = drcv[p, 0:rows, :] + keep * run
    out_4 = back(r["dsnd"], r["gin"])
    zrun = [jnp.zeros((2, 128), F32) for _ in range(SEQB)]
    for p in reversed(range(1, nch)):
        for b in range(SEQB):
            z = drcv[p, rows + 2 * b - 0 : rows + 2 * b + 2, :]
            if p < nch - 1:
                z = z + (first_of(p, b) == first_of(p + 1, b)).astype(F32) * zrun[b]
            zrun[b] = jnp.where(p > chip, z, zrun[b])
    after = jnp.minimum(chip + 1, nch - 1)
    for b in range(SEQB):
        r["gz"][2 * b : 2 * b + 2, :] = zrun[b]
        matched = (first_of(after, b) == r["info"][4 + b : 5 + b, :]) & (chip < nch - 1)
        r["last"][b] = r["last"][b] * matched.astype(F32)
    sums["q"].finish()
    sums["q"].start()
    arrived(out_4)

    def mix_last(n, carry):
        b = n // 2
        k, v, whi, w, last = r["k"][n], r["v"][n], r["whi"][n], r["w"][n], r["last"][b]
        gk = get_block(r["gin"], n, 0).astype(BF)
        gv = get_block(r["gin"], n, 1).astype(BF)
        dk = r["dkl"][n] + last * nn(whi, gk)
        dv = r["dvl"][n] + last * nn(whi, gv)
        dw = r["dwl"][n] + last * (nt(k, gk) + nt(v, gv) + r["gz"][pl.ds(n, 1), :])
        for slot, value in ((1, dk), (2, dv), (3, dw * w)):
            cols = pl.ds(pl.multiple_of(slot * 256 + lax.rem(n, 2) * 128, 128), 128)
            dd[b, :, :, cols] = value.astype(BF).reshape(2, TOK, 128)
        return carry

    lax.fori_loop(0, 4, mix_last, 0)
    tail = [sums[n] for n in ("k", "v", "x")]
    for s, lo in zip(tail, (256, 512, 768)):
        weight_gradient(lo, 256)
        s.start()

    full_q = agq[...].reshape(512, 1024)
    for b in range(SEQB):
        part = nt(dd[b].reshape(256, 1024), full_q)
        r["dn1"][:, b] = part.reshape(2, TOK, 512)
    swap_g = remote(r["dn1"].at[1 - core], r["dn1r"], mate)

    def to_rows(out_ref, height, width):
        def emit(index, value, lo=0):
            step = width // 128
            for j in range(value.shape[1] // 128):
                out_ref[pl.ds(lo // 128 + j, height, stride=step), :] = value[:, j * 128 : j * 128 + 128]

        return emit

    ends = dict(
        o=(oo_ref, 16, 512, 0), u0=(ou_ref, 16, FF, 0), u1=(ou_ref, 16, FF, 1024), d0=(od_ref, 64, 512, 0), d1=(od_ref, 64, 512, 256)
    )
    for s in ffn + [sums["o"]]:
        s.finish()
        s.start()
    for s in tail + [sums["q"]]:
        s.finish()
        s.start()
    swap_g.wait_recv()
    dn1 = (r["dn1"][core] + r["dn1r"][...]).reshape(256, 512)
    unit = r["unit1"][...]
    gains1 = jnp.sum(dn1 * unit, axis=0, keepdims=True)
    dx = r["dres"][...] + norm_back(dn1 * ga_ref[...], unit, r["inv1"][:, 0:1])
    dx_ref[...] = dx.astype(BF).reshape(SEQB, TOK, 512)

    gains = jnp.concatenate([gains1, gains2, jnp.zeros((6, 512), F32)], axis=0)

    def gain_start(ax, value):
        buf = r["gain_" + ax]
        buf[at[ax]] = value
        return [
            remote(buf.at[at[ax]], buf.at[at[ax]], device(**{ax: lax.rem(at[ax] + k, size[ax])}))
            for k in range(1, size[ax])
        ]

    def gain_finish(ax, copies):
        arrived(copies)
        buf = r["gain_" + ax]
        value = buf[0]
        for k in range(1, size[ax]):
            value = value + buf[k]
        return value

    copies = gain_start("c", gains)
    gains = gain_finish("c", copies)
    copies = gain_start("i", gains)

    for s in ffn + [sums["o"]]:
        ref, height, width, lo = ends[s.name]
        s.finish(functools.partial(to_rows(ref, height, width), lo=lo))
    gains = gain_finish("i", copies)
    copies = gain_start("a", gains)
    for s in tail:
        s.finish()
        s.start()
    gains = gain_finish("a", copies)
    copies = gain_start("o", gains)

    final, fsend = r["final"], r["fsend"]
    home = dict(q=0, k=256, v=512, x=768)
    shards = {}
    for s in [sums["q"]] + tail:
        lo = home[s.name]
        got = {}

        def keep_value(index, value, got=got):
            got[index[0]] = value

        s.finish(keep_value)
        final[core, :, lo : lo + 256] = jnp.where(first_core, got[0], got[1])
        fsend[:, lo : lo + 256] = jnp.where(first_core, got[1], got[0])
    swap_f = remote(fsend, final.at[core], mate)
    gains = gain_finish("o", copies)
    og1_ref[...] = gains[0:1]
    og2_ref[...] = gains[1:2]
    swap_f.wait_recv()
    for ref, lo in ((oq_ref, 0), (ok_ref, 256), (ov_ref, 512), (oc_ref, 768)):
        for j in range(4):
            ref[pl.ds(j, 16, stride=4), :] = final[j // 2, :, lo + (j % 2) * 128 : lo + (j % 2) * 128 + 128]
    for copy in started:
        copy.wait_send()


def solution(mesh):
    ndp, nseq = mesh.shape["dp"], mesh.shape["seq"]
    joint = D // (ndp * nseq) >= 16
    na = ndp if joint else 1
    ni = nseq // (2 * OUTER)
    scratch = layout(na, ni)
    names = tuple(scratch)
    both_axes = ("dp", "seq")

    def body(x, dy, seg, pad, *args):
        weights, (gain_attn, gain_ffn) = args[:7], args[7:]
        shards = []
        for w in weights:
            if not joint:
                whole = lax.all_gather(w, both_axes, axis=0, tiled=True).reshape(nseq, -1)
                w = lax.dynamic_index_in_dim(whole, lax.axis_index("seq"), 0, keepdims=False)
            shards.append(w.reshape(-1, 128))
        outs = [jax.ShapeDtypeStruct(x.shape, BF)] * 2
        outs += [jax.ShapeDtypeStruct(w.shape, F32) for w in shards]
        outs += [jax.ShapeDtypeStruct((1, D), F32)] * 2
        vmem = pl.BlockSpec(memory_space=pltpu.VMEM)
        got = pl.pallas_call(
            functools.partial(kernel, na, ni, names),
            out_shape=outs,
            in_specs=[vmem] * 13,
            out_specs=[vmem] * 11,
            scratch_shapes=list(scratch.values()),
            compiler_params=pltpu.CompilerParams(
                collective_id=0, has_side_effects=True, vmem_limit_bytes=62 * 2**20
            ),
            cost_estimate=pl.CostEstimate(flops=12 * 10**9, bytes_accessed=4 * 2**20, transcendentals=10**6),
            name="block",
        )(x, dy, seg, pad, *shards, gain_attn.reshape(1, D), gain_ffn.reshape(1, D))
        y, dx = got[:2]
        grads = [g.reshape(-1) for g in got[2:9]]
        gains = [g.reshape(-1) for g in got[9:]]
        if not joint:
            index = lax.axis_index("dp") * nseq + lax.axis_index("seq")
            grads = [lax.psum(g, "dp") for g in grads]
            grads = [lax.all_gather(g, "seq", axis=0, tiled=True) for g in grads]
            grads = [
                lax.dynamic_slice_in_dim(g, index * (g.shape[0] // (ndp * nseq)), g.shape[0] // (ndp * nseq))
                for g in grads
            ]
            gains = [lax.psum(g, "dp") for g in gains]
        return (y, dx, *grads, *gains)

    data, ids, flat = P("dp", "seq", None), P("dp", "seq"), P(("dp", "seq"))
    return jax.shard_map(
        body,
        mesh=mesh,
        in_specs=(data, data, ids, ids) + (flat,) * 7 + (P(), P()),
        out_specs=(data, data) + (flat,) * 7 + (P(), P()),
        check_vma=False,
    )
```

```python
import functools
import types

import jax
import jax.numpy as jnp
from jax import lax
from jax.experimental import pallas as pl
from jax.experimental.pallas import tpu as pltpu
from jax.sharding import PartitionSpec as P

D = 512
FF = 2048
TOK = 128
SEQB = 2
OUTER = 4
BF = jnp.bfloat16
F32 = jnp.float32
EPS = 1e-05
MESH = pl.DeviceIdType.MESH
AXES = "aoic"


GATHER = (
    ("agq", 768, 256, "oia"),
    ("agq", 256, 256, "oai"),
    ("agq", 512, 256, "oia"),
    ("agq", 0, 256, "oia"),
    ("ago", 0, 512, "oai"),
    ("agu", 0, 512, "ioa"),
    ("agu", 512, 512, "ioa"),
    ("agu", 1024, 512, "oai"),
    ("agu", 1536, 512, "aoi"),
    ("agd", 0, 128, "oia"),
    ("agd", 128, 128, "oai"),
    ("agd", 256, 128, "aio"),
    ("agd", 384, 128, "oia"),
)
PIECE = (
    ("gq", "aio", 0, 256, 16),
    ("gq", "iao", 256, 256, 16),
    ("gq", "aio", 512, 256, 16),
    ("gq", "aio", 768, 256, 16),
    ("go", "ciao", 0, 512, 16),
    ("gu", "ciao", 0, 512, 16),
    ("gu", "cioa", 512, 512, 16),
    ("gu", "caoi", 1024, 512, 16),
    ("gu", "caio", 1536, 512, 16),
    ("gd", "cioa", 0, 128, 64),
    ("gd", "caoi", 128, 128, 64),
    ("gd", "coia", 256, 128, 64),
    ("gd", "cioa", 384, 128, 64),
)
SCHEDULE = (
    (10, 11, 4, 8, 0, 1, 2, 5, 6, 10, 3, 0, 1, 4, 7, 2, 5, 0),
    (3, 12, 1, 2, 4, 6, 10, 9, 3, 8, 0),
    (1,),
    (),
    (2,),
    (),
    (),
    (5, 6, 12, 11, 3, 7),
    (10, 9),
    (),
    (),
    (),
    (5, 8, 12, 4),
    (6, 7, 6, 9, 4, 5, 11),
    (),
    (),
    (7, 8),
    (),
    (12,),
    (10, 9, 11),
    (7,),
    (11, 8, 12, 9),
    (),
    (24,),
    (22, 19, 23),
    (),
    (),
    (),
    (19, 24, 22, 23, 25),
    (),
    (21,),
    (),
    (20,),
    (25, 17, 19, 21, 18),
    (),
    (),
    (),
    (),
    (17, 20, 23),
    (13, 19, 21, 22),
    (),
    (),
    (14, 17),
    (20,),
    (16,),
    (13,),
    (25, 24, 15),
    (18,),
    (21, 14, 16),
    (17,),
    (24, 22, 23, 13, 15, 25),
    (18, 14, 16, 15, 21),
    (19, 25, 18, 14, 23, 20, 16, 24),
    (17, 15, 13, 22),
    (),
    (),
    (20, 18),
)


def nn(a, b):
    return jnp.dot(a, b, preferred_element_type=F32)


def nt(a, b):
    return lax.dot_general(a, b, (((1,), (1,)), ((), ())), preferred_element_type=F32)


def tn(a, b):
    return lax.dot_general(a, b, (((0,), (0,)), ((), ())), preferred_element_type=F32)


def halves(v):
    high = v.astype(BF)
    return high, (v - high.astype(F32)).astype(BF)


def norm_rows(v):
    center = v - jnp.mean(v, axis=-1, keepdims=True)
    inv = lax.rsqrt(jnp.mean(center * center, axis=-1, keepdims=True) + EPS)
    return center * inv, inv


def norm_back(g, unit, inv):
    return inv * (
        g - jnp.mean(g, axis=-1, keepdims=True) - unit * jnp.mean(g * unit, axis=-1, keepdims=True)
    )


def layout(na, ni):
    nch = OUTER * ni
    rows = 512 // nch
    lead = (na, OUTER, ni, 2)
    s = {}

    def vm(name, shape, dtype):
        s[name] = pltpu.VMEM(tuple(shape), dtype)

    vm("tmp", (256, 128), F32)
    vm("agq", lead + (16, 1024), BF)
    vm("sendq", (16, 1024), BF)
    vm("ago", lead + (16, 512), BF)
    vm("agu", lead + (16, FF), BF)
    vm("agd", lead + (64, 512), BF)
    vm("unit1", (256, 512), F32)
    vm("inv1", (256, 128), F32)
    vm("norm1", (SEQB, 2, TOK, 512), BF)
    vm("mini", (2, 8, 128), F32)
    for m in ("mask", "maskt"):
        vm(m, (SEQB, 256, 256), F32)
    for m in ("last", "use", "padb"):
        vm(m, (SEQB, 256, 128), F32)
    for m in ("q", "k", "v", "whi", "wlo"):
        vm(m, (4, 256, 128), BF)
    for m in ("w", "num", "tot", "share", "score", "dtot", "dkl", "dvl", "dwl"):
        vm(m, (4, 256, 128), F32)
    vm("dnum", (4, 256, 128), BF)
    vm("info", (8, 128), F32)
    for m, kind, extra in (("sloc", F32, 8), ("rcv", F32, 8), ("dloc", BF, 16), ("drcv", BF, 16)):
        vm(m, (nch, rows + extra, 128), kind)
    for m, kind in (("snd", F32), ("stin", F32), ("dsnd", BF), ("gin", BF)):
        vm(m, (nch, rows, 128), kind)
    vm("zin", (8, 128), F32)
    vm("gz", (8, 128), F32)
    vm("outb", (4, 2, TOK, 128), BF)
    vm("mixx", (2, 4, TOK, 128), BF)
    vm("mixed", (256, 512), BF)
    for m in ("res", "unit2", "dn2", "dres"):
        vm(m, (256, 512), F32)
    vm("inv2", (256, 128), F32)
    vm("n2", (256, 512), BF)
    vm("n2t", (512, 256), BF)
    vm("norm1t", (512, 512), BF)
    vm("hidden", (256, FF), BF)
    vm("dsilu", (256, FF), F32)
    vm("xv", (SEQB, TOK, 512), BF)
    vm("dyv", (SEQB, TOK, 512), BF)
    for name, lines in (("wq", 64), ("wk", 64), ("wv", 64), ("wc", 64), ("wo", 64), ("wu", 256), ("wd", 256)):
        vm(name, (lines, 128), BF)
    vm("do", (4, 2, TOK, 128), BF)
    vm("senddo", (4, TOK, 128), BF)
    vm("dd", (SEQB, 2, TOK, 1024), BF)
    vm("dn1", (2, SEQB, TOK, 512), F32)
    vm("dn1r", (SEQB, TOK, 512), F32)
    vm("gq", lead + (16, 1024), BF)
    vm("go", lead + (16, 512), BF)
    vm("gu", lead + (16, FF), BF)
    vm("gd", lead + (64, 512), BF)
    vm("final", (2, 16, 1024), F32)
    vm("fsend", (16, 1024), F32)
    for name, size in (("gain1", 2), ("gain2", nch), ("gain3", na)):
        vm(name, (size, 8, 128), F32)
    for name, (_, order, _, width, height) in enumerate(PIECE):
        dims = list(AXES)
        for step, ax in enumerate(order):
            size = dict(a=na, o=OUTER, i=ni, c=2)
            dims.remove(ax)
            left = tuple(size[d] for d in dims)
            vm(f"r{name}_{step}", (max(size[ax] - 1, 1),) + left + (height, width), BF)
            if step < len(order) - 1:
                vm(f"s{name}_{step}", left + (height, width), BF)
    s["load"] = pltpu.SemaphoreType.DMA((9,))
    s["sems"] = pltpu.SemaphoreType.DMA((2 * 200,))
    return s


def kernel(na, ni, names, *refs):
    (x_ref, dy_ref, seg_ref, pad_ref, wq_ref, wk_ref, wv_ref, wc_ref, wo_ref, wu_ref, wd_ref) = refs[:11]
    ga_ref, gf_ref = refs[11:13]
    (y_ref, dx_ref, oq_ref, ok_ref, ov_ref, oc_ref, oo_ref, ou_ref, od_ref, og1_ref, og2_ref) = refs[13:24]
    r = types.SimpleNamespace(**dict(zip(names, refs[24:], strict=True)))
    nch = OUTER * ni
    rows = 512 // nch
    per = 64 // rows

    dp = lax.axis_index("dp")
    seq = lax.axis_index("seq")
    chip = seq // 2
    at = dict(a=dp if na > 1 else 0, o=chip // ni, i=lax.rem(chip, ni), c=lax.rem(seq, 2))
    size = dict(a=na, o=OUTER, i=ni, c=2)
    core = at["c"]

    def device(**moved):
        p = {**at, **moved}
        return (p["a"] if na > 1 else dp, (p["o"] * ni + p["i"]) * 2 + p["c"])

    def chip_device(t):
        return (dp, t * 2 + core)

    started = []
    sems = r.sems

    def remote(src, dst, dev):
        n = len(started)
        copy = pltpu.make_async_remote_copy(
            src_ref=src,
            dst_ref=dst,
            send_sem=sems.at[2 * n],
            recv_sem=sems.at[2 * n + 1],
            device_id=dev,
            device_id_type=MESH,
        )
        copy.start()
        started.append(copy)
        return copy

    def arrived(copies):
        for copy in copies:
            copy.wait_recv()

    mate = device(c=1 - core)

    barrier = pltpu.get_barrier_semaphore()
    greet = [mate] + [chip_device(lax.rem(chip + k, nch)) for k in range(1, nch)]
    greet += [device(a=lax.rem(at["a"] + k, na)) for k in range(1, na)]
    for dev in greet:
        pl.semaphore_signal(barrier, inc=1, device_id=dev, device_id_type=MESH)

    load = {}
    for name, ref in (
        ("wq", wq_ref), ("wk", wk_ref), ("wv", wv_ref), ("wc", wc_ref), ("xv", x_ref),
        ("wo", wo_ref), ("wu", wu_ref), ("wd", wd_ref), ("dy", dy_ref),
    ):
        held = getattr(r, "dyv" if name == "dy" else name)
        load[name] = pltpu.make_async_copy(ref, held, r.load.at[len(load)])
        load[name].start()
    xv, dyv = r.xv, r.dyv

    lane = lax.broadcasted_iota(jnp.int32, (1, 128), 1)
    low = (lane < 64).astype(F32)
    high = 1.0 - low
    lowb, highb = low.astype(BF), high.astype(BF)
    hm = (lowb, highb)
    first_core = core == 0

    tmp = r.tmp

    def unpack(name, height, width):
        load[name].wait()
        ref = getattr(r, name)
        lines = height * width // 128
        tmp[0:lines, :] = ref[...].astype(F32)
        step = width // 128
        return [tmp[pl.ds(j, height, stride=step), :].astype(BF) for j in range(step)]

    own = (at["a"], at["o"], at["i"], core)
    agq, ago, agu, agd = r.agq, r.ago, r.agu, r.agd
    for w, ref in enumerate(("wq", "wk", "wv", "wc")):
        blk = unpack(ref, 16, 512)
        for j in range(2):
            cols = slice(w * 256 + j * 128, w * 256 + j * 128 + 128)
            agq[own + (slice(None), cols)] = jnp.where(first_core, blk[j], blk[2 + j])
            r.sendq[:, cols] = jnp.where(first_core, blk[2 + j], blk[j])
    for ref, buf, height, width in (("wo", ago, 16, 512), ("wu", agu, 16, FF), ("wd", agd, 64, 512)):
        for j, blk in enumerate(unpack(ref, height, width)):
            buf[own + (slice(None), slice(j * 128, j * 128 + 128))] = blk

    load["xv"].wait()
    x = xv[...].reshape(256, 512).astype(F32)
    unit, inv = norm_rows(x)
    r.unit1[...] = unit
    r.inv1[...] = jnp.broadcast_to(inv, (256, 128))
    n1own = (unit * ga_ref[...]).astype(BF)
    norm1 = r.norm1
    for b in range(SEQB):
        norm1[b, core] = n1own[b * TOK : (b + 1) * TOK]
    mini = r.mini
    mini[core, 0:2, :] = seg_ref[...].astype(F32)
    mini[core, 2:4, :] = pad_ref[...].astype(F32)
    mini[core, 4:8, :] = jnp.zeros((4, 128), F32)

    pl.semaphore_wait(barrier, len(greet))

    swap_w = remote(r.sendq, agq.at[own], mate)
    swap_m = remote(mini.at[core], mini.at[core], mate)
    swap_n = remote(norm1.at[:, core], norm1.at[:, core], mate)

    def gather(buf, axis, done, lo, width):
        cols = pl.ds(lo, width)
        index = tuple(slice(None) if d in done else pl.ds(at[d], 1) for d in AXES)
        ref = buf.at[index + (slice(None), cols)]
        return [
            remote(ref, ref, device(**{axis: lax.rem(at[axis] + k, size[axis])}))
            for k in range(1, size[axis])
        ]

    swap_w.wait_recv()
    flying, done = {}, ["c" if part[0] == "agq" else "" for part in GATHER]

    def go_on(n):
        buf, lo, width, order = GATHER[n]
        if n in flying:
            arrived(flying.pop(n))
        left = [d for d in order + "c" if d not in done[n]]
        if left:
            flying[n] = gather(getattr(r, buf), left[0], done[n], lo, width)
            done[n] += left[0]

    sums = []

    agenda = iter(SCHEDULE)

    def point():
        for n in next(agenda):
            if n < len(GATHER):
                go_on(n)
            else:
                sums[n - len(GATHER)].advance()

    point()
    arrived([swap_m, swap_n])
    point()
    r.norm1t[...] = norm1[...].reshape(512, 512).T

    turned = [mini[s].T for s in range(2)]
    big_row = lax.broadcasted_iota(jnp.int32, (256, 256), 0)
    big_col = lax.broadcasted_iota(jnp.int32, (256, 256), 1)
    for b in range(SEQB):
        seg_row = jnp.concatenate([mini[0, b : b + 1, :], mini[1, b : b + 1, :]], axis=1)
        seg_col = jnp.concatenate([t[:, b : b + 1] for t in turned], axis=0)
        pad_col = jnp.concatenate([t[:, 2 + b : 3 + b] for t in turned], axis=0)
        same = seg_col == seg_row
        r.mask[b] = jnp.where(same & (big_row >= big_col), 1.0, 0.0)
        r.maskt[b] = jnp.where(same & (big_row <= big_col), 1.0, 0.0)
        seg_last = seg_row[:, 255:256]
        r.last[b] = jnp.broadcast_to((seg_col == seg_last).astype(F32), (256, 128))
        r.padb[b] = jnp.broadcast_to(pad_col, (256, 128))
        r.info[4 + b : 5 + b, :] = jnp.broadcast_to(seg_last, (1, 128))
        r.info[6 + b : 7 + b, :] = jnp.broadcast_to(seg_row[:, 0:1], (1, 128))

    def project(w):
        point()
        mat = agq[..., w * 256 : w * 256 + 256].reshape(512, 256)
        for b in range(SEQB):
            out = nn(norm1[b].reshape(256, 512), mat)
            for pair in range(2):
                part = out[:, pair * 128 : pair * 128 + 128]
                n = b * 2 + pair
                if w == 3:
                    weight = jnp.exp(part) * r.padb[b]
                    r.w[n] = weight
                    r.whi[n], r.wlo[n] = halves(weight)
                else:
                    (r.q, r.k, r.v)[w][n] = part.astype(BF)

    for w in (3, 1, 2):
        project(w)

    def fold(full):
        return full[0:64] * low + full[64:128] * high

    def put_state(ref, n, which, value):
        for t in range(per):
            ref[(n * 2 + which) * per + t, 0:rows, :] = value[t * rows : (t + 1) * rows].astype(ref.dtype)

    def get_block(ref, n, which):
        value = ref[pl.ds((n * 2 + which) * per, per)].astype(F32).reshape(64, 128)
        return jnp.concatenate([value * low, value * high], axis=0)

    def local_state(n, carry):
        weight = r.w[n] * r.last[n // 2]
        hi, lo = halves(weight)
        for which, rhs in enumerate((r.k[n], r.v[n])):
            put_state(r.sloc, n, which, fold(tn(hi, rhs) + tn(lo, rhs)))
        r.info[pl.ds(n, 1), :] = jnp.sum(weight, axis=0, keepdims=True)
        return carry

    point()
    lax.fori_loop(0, 4, local_state, 0)

    def spread(src, dst, info):
        for t in range(nch):
            src[t, rows:, :] = info
        dst[chip] = src[chip]
        return [
            remote(src.at[lax.rem(chip + k, nch)], dst.at[chip], chip_device(lax.rem(chip + k, nch)))
            for k in range(1, nch)
        ]

    def back(src, dst):
        dst[chip] = src[chip]
        return [
            remote(src.at[lax.rem(chip + k, nch)], dst.at[chip], chip_device(lax.rem(chip + k, nch)))
            for k in range(1, nch)
        ]

    point()
    out_1 = spread(r.sloc, r.rcv, r.info[...])

    project(0)

    def mix_local(n, carry):
        q, k, whi, wlo = r.q[n], r.k[n], r.whi[n], r.wlo[n]
        mask = r.mask[n // 2]
        num = jnp.zeros((256, 128), F32)
        for m in hm:
            hi, lo = halves(nt(q * m, k) * mask)
            num += nn(hi, whi * m) + nn(lo, whi * m) + nn(hi, wlo * m)
        r.num[n] = num
        maskb = mask.astype(BF)
        r.tot[n] = nn(maskb, whi) + nn(maskb, wlo)
        return carry

    point()
    lax.fori_loop(0, 4, mix_local, 0)
    point()

    arrived(out_1)
    point()
    rcv = r.rcv
    owned = (chip * rows) // 256

    def last_of(p, b):
        return rcv[p, pl.ds(rows + 4 + b, 1), :]

    def first_of(p, b):
        return rcv[p, pl.ds(rows + 6 + b, 1), :]

    run = jnp.zeros((rows, 128), F32)
    for p in range(nch):
        r.snd[p] = run
        if p == 0:
            run = rcv[0, 0:rows, :]
        else:
            keep = (last_of(p - 1, owned) == last_of(p, owned)).astype(F32)
            run = rcv[p, 0:rows, :] + keep * run
    point()
    out_2 = back(r.snd, r.stin)
    point()
    zrun = [jnp.zeros((2, 128), F32) for _ in range(SEQB)]
    for p in range(nch - 1):
        for b in range(SEQB):
            z = rcv[p, rows + 2 * b : rows + 2 * b + 2, :]
            if p > 0:
                z = z + (last_of(p - 1, b) == last_of(p, b)).astype(F32) * zrun[b]
            zrun[b] = jnp.where(p < chip, z, zrun[b])
    before = jnp.maximum(chip - 1, 0)
    for b in range(SEQB):
        r.zin[2 * b : 2 * b + 2, :] = zrun[b]
        open_doc = jnp.where(chip > 0, last_of(before, b), -1.0)[:, 0:1]
        seg_col = jnp.concatenate([t[:, b : b + 1] for t in turned], axis=0)
        r.use[b] = jnp.broadcast_to((seg_col == open_doc).astype(F32), (256, 128))

    point()
    arrived(out_2)

    def both(op, v):
        if op is jnp.max:
            a = jnp.max(jnp.where(lane < 64, v, -jnp.inf), axis=1, keepdims=True)
            b = jnp.max(jnp.where(lane < 64, -jnp.inf, v), axis=1, keepdims=True)
        else:
            a = jnp.sum(v * low, axis=1, keepdims=True)
            b = jnp.sum(v * high, axis=1, keepdims=True)
        return jnp.where(lane < 64, a, b)

    def mix_rest(n, carry):
        b = n // 2
        q, v, whi = r.q[n], r.v[n], r.whi[n]
        mask, use = r.mask[b], r.use[b]
        khi, klo = halves(get_block(r.stin, n, 0))
        num = r.num[n] + use * (nt(q, khi) + nt(q, klo))
        tot = r.tot[n] + use * r.zin[pl.ds(n, 1), :]
        floor = jnp.maximum(tot, 1.0)
        score = num / (floor * 8.0)
        e = jnp.exp(score - both(jnp.max, score))
        share = e / (both(jnp.sum, e) * floor)
        r.tot[n] = tot
        r.score[n] = score
        r.share[n] = share
        sb = share.astype(BF)
        out = use * nn(sb, get_block(r.stin, n, 1).astype(BF))
        for m in hm:
            out += nn((nt(sb * m, whi) * mask).astype(BF), v * m)
        r.outb[n] = out.astype(BF).reshape(2, TOK, 128)
        return carry

    point()
    lax.fori_loop(0, 4, mix_rest, 0)
    point()
    swap_o = remote(r.outb.at[:, 1 - core], r.mixx.at[core], mate)
    for n in range(4):
        r.mixx[core, n] = r.outb[n, core]

    point()
    swap_o.wait_recv()
    point()
    mixx = r.mixx
    for b in range(SEQB):
        r.mixed[b * TOK : (b + 1) * TOK, :] = jnp.concatenate(
            [mixx[h, b * 2 + p] for h in range(2) for p in range(2)], axis=1
        )
    w_out = ago[...].reshape(512, 512)
    residual = xv[...].reshape(256, 512).astype(F32) + nn(r.mixed[...], w_out)
    r.res[...] = residual
    unit, inv = norm_rows(residual)
    r.unit2[...] = unit
    r.inv2[...] = jnp.broadcast_to(inv, (256, 128))
    r.n2[...] = (unit * gf_ref[...]).astype(BF)
    r.n2t[...] = r.n2[...].T

    class Sum:
        def __init__(self, name, buffer, order, width, height, lo, emit):
            self.emit = emit
            self.name, self.order, self.width, self.height = name, order, width, height
            self.ref, self.lo, self.dims, self.step = getattr(r, buffer), lo, list(AXES), 0
            self.going = False

        def start(self):
            ax = self.order[self.step]
            p = self.dims.index(ax)
            cols = pl.ds(self.lo, self.width)
            land = getattr(r, f"r{self.name}_{self.step}")
            self.copies, self.going = [], True
            for k in range(1, size[ax]):
                to = lax.rem(at[ax] + k, size[ax])
                index = [slice(None)] * len(self.dims) + [slice(None), cols]
                index[p] = to
                self.copies.append(remote(self.ref.at[tuple(index)], land.at[k - 1], device(**{ax: to})))

        def advance(self):
            if self.going:
                self.finish()
            if self.step < len(self.order):
                self.start()

        def finish(self):
            emit = self.emit if self.step == len(self.order) - 1 else None
            ax = self.order[self.step]
            p = self.dims.index(ax)
            arrived(self.copies)
            land = getattr(r, f"r{self.name}_{self.step}")
            cols = slice(self.lo, self.lo + self.width)
            left = [size[d] for d in self.dims if d != ax]
            total = 1
            for extent in left:
                total *= extent
            into = None if emit else getattr(r, f"s{self.name}_{self.step}")

            def one(flat):
                index, rest_of = [], flat
                for extent in reversed(left):
                    index.insert(0, rest_of % extent if isinstance(rest_of, int) else lax.rem(rest_of, extent))
                    rest_of = rest_of // extent
                full = list(index)
                full.insert(p, at[ax])
                value = self.ref[tuple(full) + (slice(None), cols)].astype(F32)
                for k in range(size[ax] - 1):
                    value += land[(k,) + tuple(index)].astype(F32)
                if emit:
                    emit(index, value)
                else:
                    into[tuple(index)] = value.astype(BF)

            if total <= 2:
                for flat in range(total):
                    one(flat)
            else:
                def body(flat, carry):
                    one(flat)
                    return carry

                lax.fori_loop(0, total, body, 0)
            self.dims.remove(ax)
            self.ref, self.lo, self.step = into, 0, self.step + 1

    def to_rows(out_ref, height, width, lo):
        def emit(index, value):
            step = width // 128
            for j in range(value.shape[1] // 128):
                out_ref[pl.ds(lo // 128 + j, height, stride=step), :] = value[:, j * 128 : j * 128 + 128]

        return emit

    shards = {}

    def to_core(name):
        def emit(index, value):
            shards[name, index[0]] = value
            if index[0] == 1:
                at_lo = slice(PIECE[name][2], PIECE[name][2] + 256)
                halves_of = (shards[name, 0], shards[name, 1])
                r.final[core, :, at_lo] = jnp.where(first_core, *halves_of)
                r.fsend[:, at_lo] = jnp.where(first_core, *reversed(halves_of))

        return emit

    outs = dict(go=(oo_ref, 16, 512), gu=(ou_ref, 16, FF), gd=(od_ref, 64, 512))
    for name, (buf, order, lo, width, height) in enumerate(PIECE):
        emit = to_core(name) if buf == "gq" else to_rows(*outs[buf], lo)
        sums.append(Sum(name, buf, order, width, height, lo, emit))

    load["dy"].wait()
    dy = dyv[...].reshape(256, 512)
    span = na * OUTER // 4
    for j in range(4):
        point()
        cols = slice(j * 512, j * 512 + 512)
        pre = nn(r.n2[...], agu[:, :, :, :, :, cols].reshape(512, 512))
        sig = 1.0 / (1.0 + jnp.exp(-pre))
        hidden = (pre * sig).astype(BF)
        r.hidden[:, cols] = hidden
        r.dsilu[:, cols] = sig * (1.0 + pre * (1.0 - sig))
        block = (j * span // OUTER, slice(j * span % OUTER, j * span % OUTER + span))
        r.gd[block] = tn(hidden, dy).astype(BF).reshape((span, ni, 2, 64, 512))
    for j in range(4):
        point()
        cols = slice(j * 512, j * 512 + 512)
        block = (j * span // OUTER, slice(j * span % OUTER, j * span % OUTER + span))
        d_pre = (nt(dy, agd[block].reshape(512, 512)) * r.dsilu[:, cols]).astype(BF)
        part = nt(d_pre, agu[:, :, :, :, :, cols].reshape(512, 512))
        r.dn2[...] = part if j == 0 else r.dn2[...] + part
        r.gu[:, :, :, :, :, cols] = nn(r.n2t[...], d_pre).astype(BF).reshape((na, OUTER, ni, 2, 16, 512))
    point()

    dn2 = r.dn2[...]
    unit = r.unit2[...]
    gains2 = jnp.sum(dn2 * unit, axis=0, keepdims=True)
    d_res = dy.astype(F32) + norm_back(
        dn2 * gf_ref[...], unit, r.inv2[:, 0:1]
    )
    r.dres[...] = d_res
    d_attn = d_res.astype(BF)
    d_mixed = nt(d_attn, w_out).astype(BF)
    for b in range(SEQB):
        for p in range(2):
            part = [d_mixed[b * TOK : (b + 1) * TOK, h * 256 + p * 128 : h * 256 + p * 128 + 128] for h in range(2)]
            r.do[b * 2 + p, core] = jnp.where(first_core, part[0], part[1])
            r.senddo[b * 2 + p] = jnp.where(first_core, part[1], part[0])
    point()
    swap_d = remote(r.senddo, r.do.at[:, core], mate)
    point()
    swap_d.wait_recv()

    def mix_back(n, carry):
        b = n // 2
        q, v, whi = r.q[n], r.v[n], r.whi[n]
        mask, use = r.mask[b], r.use[b]
        share, tot, score = r.share[n], r.tot[n], r.score[n]
        d_out = r.do[n].reshape(256, 128)
        ds = use * nt(d_out, get_block(r.stin, n, 1).astype(BF))
        for m in hm:
            ds += nn((nt(d_out * m, v) * mask).astype(BF), whi * m)
        floor = jnp.maximum(tot, 1.0)
        inv_floor = 1.0 / floor
        prob = share * floor
        dprob = ds * inv_floor
        dscore = prob * (dprob - both(jnp.sum, dprob * prob))
        dnum = dscore * inv_floor * 0.125
        gate = jnp.where(tot > 1.0, 1.0, jnp.where(tot == 1.0, 0.5, 0.0))
        dtot = -(ds * share + dscore * score) * inv_floor * gate
        r.dnum[n] = dnum.astype(BF)
        r.dtot[n] = dtot
        put_state(r.dloc, n, 0, fold(tn((use * dnum).astype(BF), q)))
        put_state(r.dloc, n, 1, fold(tn((use * share).astype(BF), d_out)))
        r.gz[pl.ds(n, 1), :] = jnp.sum(use * dtot, axis=0, keepdims=True)
        return carry

    point()
    lax.fori_loop(0, 4, mix_back, 0)
    point()
    r.gz[4:8, :] = jnp.zeros((4, 128), F32)
    gz_parts = jnp.concatenate(halves(r.gz[...]), axis=0)
    out_3 = spread(r.dloc, r.drcv, gz_parts)

    point()
    r.go[...] = tn(r.mixed[...], d_attn).astype(BF).reshape((na, OUTER, ni, 2, 16, 512))
    point()
    y_rows = r.res[...] + nn(r.hidden[...], agd[...].reshape(FF, 512))
    y_ref[...] = y_rows.astype(BF).reshape(SEQB, TOK, 512)

    def mix_back_local(n, carry):
        b = n // 2
        q, k, v, whi, w = r.q[n], r.k[n], r.v[n], r.whi[n], r.w[n]
        mask, maskt, use = r.mask[b], r.maskt[b], r.use[b]
        d_out, dnum = r.do[n].reshape(256, 128), r.dnum[n]
        sb = r.share[n].astype(BF)
        dq = use * nn(dnum, get_block(r.stin, n, 0).astype(BF))
        dk = jnp.zeros((256, 128), F32)
        dv = jnp.zeros((256, 128), F32)
        dw = nn(maskt.astype(BF), r.dtot[n].astype(BF))
        for m in hm:
            dq += nn((nt(dnum * m, whi) * mask).astype(BF), k * m)
            dk += nn((nt(whi * m, dnum) * maskt).astype(BF), q * m)
            dv += nn((nt(whi * m, sb) * maskt).astype(BF), d_out * m)
            dw += nn((nt(v * m, d_out) * maskt).astype(BF), sb * m)
            dw += nn((nt(k * m, q) * maskt).astype(BF), dnum * m)
        cols = pl.ds(pl.multiple_of(lax.rem(n, 2) * 128, 128), 128)
        r.dd[b, :, :, cols] = dq.astype(BF).reshape(2, TOK, 128)
        r.dkl[n] = dk
        r.dvl[n] = dv
        r.dwl[n] = dw
        return carry

    point()
    lax.fori_loop(0, 4, mix_back_local, 0)
    dd = r.dd

    def weight_gradient(lo, width):
        value = nn(r.norm1t[...], dd[:, :, :, lo : lo + width].reshape(512, width))
        r.gq[:, :, :, :, :, lo : lo + width] = value.astype(BF).reshape((na, OUTER, ni, 2, 16, width))

    point()
    weight_gradient(0, 256)
    point()

    arrived(out_3)
    point()
    drcv = r.drcv
    run = jnp.zeros((rows, 128), F32)
    for p in reversed(range(nch)):
        r.dsnd[p] = run.astype(BF)
        here = drcv[p, 0:rows, :].astype(F32)
        if p == nch - 1:
            run = here
        else:
            run = here + (first_of(p, owned) == first_of(p + 1, owned)).astype(F32) * run
    point()
    out_4 = back(r.dsnd, r.gin)
    point()
    zrun = [jnp.zeros((2, 128), F32) for _ in range(SEQB)]
    for p in reversed(range(1, nch)):
        for b in range(SEQB):
            tail = drcv[p, rows : rows + 16, :].astype(F32)
            z = tail[2 * b : 2 * b + 2] + tail[8 + 2 * b : 10 + 2 * b]
            if p < nch - 1:
                z = z + (first_of(p, b) == first_of(p + 1, b)).astype(F32) * zrun[b]
            zrun[b] = jnp.where(p > chip, z, zrun[b])
    after = jnp.minimum(chip + 1, nch - 1)
    for b in range(SEQB):
        r.gz[2 * b : 2 * b + 2, :] = zrun[b]
        matched = (first_of(after, b) == r.info[4 + b : 5 + b, :]) & (chip < nch - 1)
        r.last[b] = r.last[b] * matched.astype(F32)
    point()
    arrived(out_4)
    point()

    def mix_last(n, carry):
        b = n // 2
        k, v, whi, w, last = r.k[n], r.v[n], r.whi[n], r.w[n], r.last[b]
        gk = get_block(r.gin, n, 0).astype(BF)
        gv = get_block(r.gin, n, 1).astype(BF)
        dk = r.dkl[n] + last * nn(whi, gk)
        dv = r.dvl[n] + last * nn(whi, gv)
        dw = r.dwl[n] + last * (nt(k, gk) + nt(v, gv) + r.gz[pl.ds(n, 1), :])
        for slot, value in ((1, dk), (2, dv), (3, dw * w)):
            cols = pl.ds(pl.multiple_of(slot * 256 + lax.rem(n, 2) * 128, 128), 128)
            dd[b, :, :, cols] = value.astype(BF).reshape(2, TOK, 128)
        return carry

    lax.fori_loop(0, 4, mix_last, 0)
    for name, lo in (("kg", 256), ("vg", 512), ("cg", 768)):
        point()
        weight_gradient(lo, 256)

    point()
    full_q = agq[...].reshape(512, 1024)
    for b in range(SEQB):
        part = nt(dd[b].reshape(256, 1024), full_q)
        r.dn1[:, b] = part.reshape(2, TOK, 512)
    point()
    swap_g = remote(r.dn1.at[1 - core], r.dn1r, mate)

    point()
    swap_g.wait_recv()
    point()
    dn1 = (r.dn1[core] + r.dn1r[...]).reshape(256, 512)
    unit = r.unit1[...]
    gains1 = jnp.sum(dn1 * unit, axis=0, keepdims=True)
    dx = r.dres[...] + norm_back(dn1 * ga_ref[...], unit, r.inv1[:, 0:1])
    dx_ref[...] = dx.astype(BF).reshape(SEQB, TOK, 512)

    gains = jnp.concatenate(
        [g[:, j * 128 : j * 128 + 128] for g in (gains1, gains2) for j in range(4)], axis=0
    )

    def exchange(buf, value, me, count, dev):
        buf[me] = value
        return [remote(buf.at[me], buf.at[me], dev(lax.rem(me + k, count))) for k in range(1, count)]

    def total(buf, copies, count):
        arrived(copies)
        value = buf[0]
        for k in range(1, count):
            value = value + buf[k]
        return value

    point()
    copies = exchange(r.gain1, gains, core, 2, lambda t: device(c=t))
    point()
    gains = total(r.gain1, copies, 2)
    point()
    copies = exchange(r.gain2, gains, chip, nch, chip_device)
    point()
    gains = total(r.gain2, copies, nch)
    point()
    copies = exchange(r.gain3, gains, at["a"], na, lambda t: device(a=t))

    final = r.final
    point()
    swap_f = remote(r.fsend, final.at[core], mate)
    point()
    gains = total(r.gain3, copies, na)
    for ref, first in ((og1_ref, 0), (og2_ref, 4)):
        for j in range(4):
            ref[:, j * 128 : j * 128 + 128] = gains[first + j : first + j + 1]
    point()
    swap_f.wait_recv()
    for ref, lo in ((oq_ref, 0), (ok_ref, 256), (ov_ref, 512), (oc_ref, 768)):
        for j in range(4):
            ref[pl.ds(j, 16, stride=4), :] = final[j // 2, :, lo + (j % 2) * 128 : lo + (j % 2) * 128 + 128]
    point()
    for copy in started:
        copy.wait_send()


def hand_over(count, *refs):
    src, dst, held, sems = refs[:count], refs[count : 2 * count], refs[2 * count : 3 * count], refs[3 * count]
    into = [pltpu.make_async_copy(src[n], held[n], sems.at[0, n]) for n in range(count)]
    away = [pltpu.make_async_copy(held[n], dst[n], sems.at[1, n]) for n in range(count)]
    for copy in into:
        copy.start()
    for n in range(count):
        into[n].wait()
        away[n].start()
    for copy in away:
        copy.wait()


def solution(mesh):
    ndp, nseq = mesh.shape["dp"], mesh.shape["seq"]
    joint = D // (ndp * nseq) >= 16
    na = ndp if joint else 1
    ni = nseq // (2 * OUTER)
    scratch = layout(na, ni)
    names = tuple(scratch)
    both_axes = ("dp", "seq")

    def body(x, dy, seg, pad, *args):
        weights, (gain_attn, gain_ffn) = args[:7], args[7:]
        shards = []
        for w in weights:
            if not joint:
                whole = lax.all_gather(w, both_axes, axis=0, tiled=True).reshape(nseq, -1)
                w = lax.dynamic_index_in_dim(whole, lax.axis_index("seq"), 0, keepdims=False)
            shards.append(w.reshape(-1, 128))
        outs = [jax.ShapeDtypeStruct(x.shape, BF)] * 2
        outs += [jax.ShapeDtypeStruct(w.shape, F32) for w in shards]
        outs += [jax.ShapeDtypeStruct((1, D), F32)] * 2
        vmem, hbm = pl.BlockSpec(memory_space=pltpu.VMEM), pl.BlockSpec(memory_space=pltpu.HBM)
        got = pl.pallas_call(
            functools.partial(kernel, na, ni, names),
            out_shape=outs,
            in_specs=[hbm] * 2 + [vmem] * 2 + [hbm] * 7 + [vmem] * 2,
            out_specs=[vmem] * 11,
            scratch_shapes=list(scratch.values()),
            compiler_params=pltpu.CompilerParams(
                collective_id=0, has_side_effects=True, vmem_limit_bytes=62 * 2**20
            ),
            cost_estimate=pl.CostEstimate(flops=12 * 10**9, bytes_accessed=4 * 2**20, transcendentals=10**6),
            name="block",
        )(x, dy, seg, pad, *shards, gain_attn.reshape(1, D), gain_ffn.reshape(1, D))
        got = pl.pallas_call(
            functools.partial(hand_over, 11),
            out_shape=outs,
            in_specs=[hbm] * 11,
            out_specs=[hbm] * 11,
            scratch_shapes=[pltpu.VMEM(o.shape, o.dtype) for o in outs] + [pltpu.SemaphoreType.DMA((2, 11))],
            name="results",
        )(*got)
        y, dx = got[:2]
        grads = [g.reshape(-1) for g in got[2:9]]
        gains = [g.reshape(-1) for g in got[9:]]
        if not joint:
            index = lax.axis_index("dp") * nseq + lax.axis_index("seq")
            grads = [lax.psum(g, "dp") for g in grads]
            grads = [lax.all_gather(g, "seq", axis=0, tiled=True) for g in grads]
            grads = [
                lax.dynamic_slice_in_dim(g, index * (g.shape[0] // (ndp * nseq)), g.shape[0] // (ndp * nseq))
                for g in grads
            ]
            gains = [lax.psum(g, "dp") for g in gains]
        return (y, dx, *grads, *gains)

    data, ids, flat = P("dp", "seq", None), P("dp", "seq"), P(("dp", "seq"))
    return jax.shard_map(
        body,
        mesh=mesh,
        in_specs=(data, data, ids, ids) + (flat,) * 7 + (P(), P()),
        out_specs=(data, data) + (flat,) * 7 + (P(), P()),
        check_vma=False,
    )
```

```python
import functools
import types

import jax
import jax.numpy as jnp
from jax import lax
from jax.experimental import pallas as pl
from jax.experimental.pallas import tpu as pltpu
from jax.sharding import PartitionSpec as P

D = 512
FF = 2048
TOK = 128
SEQB = 2
OUTER = 4
BF = jnp.bfloat16
F32 = jnp.float32
EPS = 1e-05
MESH = pl.DeviceIdType.MESH
AXES = "apric"


GATHER = (
    ("agq", 768, 256, "rpia"),
    ("agq", 256, 256, "pari"),
    ("agq", 512, 256, "rpia"),
    ("agq", 0, 256, "apri"),
    ("ago", 0, 512, "piar"),
    ("agu", 0, 512, "pira"),
    ("agu", 512, 512, "rpai"),
    ("agu", 1024, 512, "iapr"),
    ("agu", 1536, 512, "ipar"),
    ("agd", 0, 128, "pria"),
    ("agd", 128, 128, "rpai"),
    ("agd", 256, 128, "prai"),
    ("agd", 384, 128, "prai"),
)
PIECE = (
    ("gq", "iarp", 0, 256, 16),
    ("gq", "airp", 256, 256, 16),
    ("gq", "iarp", 512, 256, 16),
    ("gq", "raip", 768, 256, 16),
    ("go", "cripa", 0, 512, 16),
    ("gu", "cripa", 0, 512, 16),
    ("gu", "ciarp", 512, 512, 16),
    ("gu", "capri", 1024, 512, 16),
    ("gu", "ciapr", 1536, 512, 16),
    ("gd", "cairp", 0, 128, 64),
    ("gd", "crapi", 128, 128, 64),
    ("gd", "cripa", 256, 128, 64),
    ("gd", "caipr", 384, 128, 64),
)
SCHEDULE = (
    (0, 11, 9),
    (7, 2, 1),
    (4, 0, 11, 3, 12, 9, 6, 1, 2, 7, 3, 0, 11, 10, 9, 1, 2, 10, 0, 8, 4, 5, 3, 1, 7, 6, 2, 12, 10, 3, 8, 5, 7, 0, 4),
    (11, 1),
    (6, 2),
    (),
    (),
    (9, 7, 12, 3, 4, 5, 10, 8),
    (),
    (11,),
    (),
    (),
    (9, 5, 6, 4, 7, 9),
    (10, 4, 8, 10, 12),
    (),
    (),
    (6, 11, 5, 8, 12),
    (),
    (6, 5),
    (),
    (12,),
    (8,),
    (24,),
    (25,),
    (),
    (20,),
    (21,),
    (),
    (25, 23, 20, 24, 21),
    (),
    (),
    (18, 23),
    (),
    (),
    (),
    (),
    (24,),
    (18, 23, 19),
    (),
    (13, 22, 21, 20),
    (25, 17),
    (22, 24),
    (15,),
    (21, 17),
    (),
    (19, 14),
    (20, 16, 18),
    (13, 15),
    (25, 17, 14),
    (21, 19, 23),
    (),
    (),
    (),
    (24, 15, 16, 22, 13, 18, 17, 20, 14),
    (19, 15, 16, 13, 22, 14, 25, 18),
    (19, 16, 24, 22, 15, 17, 23, 21, 14, 13, 20, 16),
    (19, 17, 23, 25, 18),
    (),
    (22,),
)


def nn(a, b):
    return jnp.dot(a, b, preferred_element_type=F32)


def nt(a, b):
    return lax.dot_general(a, b, (((1,), (1,)), ((), ())), preferred_element_type=F32)


def tn(a, b):
    return lax.dot_general(a, b, (((0,), (0,)), ((), ())), preferred_element_type=F32)


def halves(v):
    high = v.astype(BF)
    return high, (v - high.astype(F32)).astype(BF)


def norm_rows(v):
    center = v - jnp.mean(v, axis=-1, keepdims=True)
    inv = lax.rsqrt(jnp.mean(center * center, axis=-1, keepdims=True) + EPS)
    return center * inv, inv


def norm_back(g, unit, inv):
    return inv * (
        g - jnp.mean(g, axis=-1, keepdims=True) - unit * jnp.mean(g * unit, axis=-1, keepdims=True)
    )


def layout(na, ni):
    nch = OUTER * ni
    rows = 512 // nch
    lead = (na, 2, 2, ni, 2)
    s = {}

    def vm(name, shape, dtype):
        s[name] = pltpu.VMEM(tuple(shape), dtype)

    vm("tmp", (256, 128), F32)
    vm("agq", lead + (16, 1024), BF)
    vm("sendq", (16, 1024), BF)
    vm("ago", lead + (16, 512), BF)
    vm("agu", lead + (16, FF), BF)
    vm("agd", lead + (64, 512), BF)
    vm("unit1", (SEQB, 2, TOK, 512), F32)
    vm("inv1", (SEQB, 2, TOK, 128), F32)
    vm("norm1", (SEQB, 2, TOK, 512), BF)
    vm("mini", (2, 8, 128), F32)
    for m in ("mask", "maskt"):
        vm(m, (SEQB, 256, 256), F32)
    for m in ("last", "use", "padb"):
        vm(m, (SEQB, 256, 128), F32)
    for m in ("q", "k", "v", "whi", "wlo"):
        vm(m, (4, 256, 128), BF)
    for m in ("w", "num", "tot", "share", "score", "dtot", "dkl", "dvl", "dwl"):
        vm(m, (4, 256, 128), F32)
    vm("dnum", (4, 256, 128), BF)
    vm("info", (8, 128), F32)
    for m, kind, extra in (("dloc", BF, 16), ("drcv", BF, 16)):
        vm(m, (nch, rows + extra, 128), kind)
    for m in ("dsnd", "gin"):
        vm(m, (nch, rows, 128), BF)
    third = 256 // nch
    for m, extra in (("sloc", 16), ("rcv", 16), ("snd", 0), ("stin", 0)):
        vm(m, (nch, 3 * third + extra, 128), BF)
    vm("infos", (nch, 8, 128), F32)
    vm("zin", (8, 128), F32)
    vm("gz", (8, 128), F32)
    vm("outb", (4, 2, TOK, 128), BF)
    vm("mixx", (2, 4, TOK, 128), BF)
    vm("mixed", (256, 512), BF)
    for m in ("res", "unit2", "dn2", "dres"):
        vm(m, (256, 512), F32)
    vm("inv2", (256, 128), F32)
    vm("n2", (256, 512), BF)
    vm("n2t", (512, 256), BF)
    vm("norm1t", (512, 512), BF)
    vm("hidden", (256, FF), BF)
    vm("dsilu", (256, FF), F32)
    vm("xall", (SEQB, 2, TOK, 512), BF)
    vm("dyv", (SEQB, TOK, 512), BF)
    for name, lines in (("wq", 64), ("wk", 64), ("wv", 64), ("wc", 64), ("wo", 64), ("wu", 256), ("wd", 256)):
        vm(name, (lines, 128), BF)
    vm("do", (4, 2, TOK, 128), BF)
    vm("senddo", (4, TOK, 128), BF)
    vm("dd", (SEQB, 2, TOK, 1024), BF)
    vm("dn1", (2, SEQB, TOK, 512), F32)
    vm("dn1r", (SEQB, TOK, 512), F32)
    vm("gq", lead + (16, 1024), BF)
    vm("go", lead + (16, 512), BF)
    vm("gu", lead + (16, FF), BF)
    vm("gd", lead + (64, 512), BF)
    vm("final", (2, 16, 1024), F32)
    vm("fsend", (16, 1024), F32)
    for name, size in (("gain1", 2), ("gain2", nch), ("gain3", na)):
        vm(name, (size, 8, 128), F32)
    for name, (_, order, _, width, height) in enumerate(PIECE):
        dims = list(AXES)
        for step, ax in enumerate(order):
            size = dict(a=na, p=2, r=2, i=ni, c=2)
            dims.remove(ax)
            left = tuple(size[d] for d in dims)
            vm(f"r{name}_{step}", (max(size[ax] - 1, 1),) + left + (height, width), BF)
            if step < len(order) - 1:
                vm(f"s{name}_{step}", left + (height, width), BF)
    s["load"] = pltpu.SemaphoreType.DMA((9,))
    s["sems"] = pltpu.SemaphoreType.DMA((2 * 200,))
    return s


def kernel(na, ni, names, *refs):
    (x_ref, dy_ref, seg_ref, pad_ref, wq_ref, wk_ref, wv_ref, wc_ref, wo_ref, wu_ref, wd_ref) = refs[:11]
    ga_ref, gf_ref = refs[11:13]
    (y_ref, dx_ref, oq_ref, ok_ref, ov_ref, oc_ref, oo_ref, ou_ref, od_ref, og1_ref, og2_ref) = refs[13:24]
    r = types.SimpleNamespace(**dict(zip(names, refs[24:], strict=True)))
    nch = OUTER * ni
    rows = 512 // nch
    per = 64 // rows
    third = 256 // nch
    share_of = 64 // third

    dp = lax.axis_index("dp")
    seq = lax.axis_index("seq")
    chip = seq // 2
    at = dict(
        a=dp if na > 1 else 0,
        p=chip // (2 * ni),
        r=lax.rem(chip // ni, 2),
        i=lax.rem(chip, ni),
        c=lax.rem(seq, 2),
    )
    size = dict(a=na, p=2, r=2, i=ni, c=2)
    lead = (na, 2, 2, ni, 2)
    core = at["c"]

    def device(**moved):
        p = {**at, **moved}
        return (p["a"] if na > 1 else dp, ((p["p"] * 2 + p["r"]) * ni + p["i"]) * 2 + p["c"])

    def chip_device(t):
        return (dp, t * 2 + core)

    started = []
    sems = r.sems

    def remote(src, dst, dev):
        n = len(started)
        copy = pltpu.make_async_remote_copy(
            src_ref=src,
            dst_ref=dst,
            send_sem=sems.at[2 * n],
            recv_sem=sems.at[2 * n + 1],
            device_id=dev,
            device_id_type=MESH,
        )
        copy.start()
        started.append(copy)
        return copy

    def arrived(copies):
        for copy in copies:
            copy.wait_recv()

    mate = device(c=1 - core)

    barrier = pltpu.get_barrier_semaphore()
    greet = [mate] + [chip_device(lax.rem(chip + k, nch)) for k in range(1, nch)]
    greet += [device(a=lax.rem(at["a"] + k, na)) for k in range(1, na)]
    for dev in greet:
        pl.semaphore_signal(barrier, inc=1, device_id=dev, device_id_type=MESH)

    load = {}
    for name, ref in (
        ("wq", wq_ref), ("wk", wk_ref), ("wv", wv_ref), ("wc", wc_ref), ("x", x_ref),
        ("wo", wo_ref), ("wu", wu_ref), ("wd", wd_ref), ("dy", dy_ref),
    ):
        held = r.xall.at[:, core] if name == "x" else r.dyv if name == "dy" else getattr(r, name)
        load[name] = pltpu.make_async_copy(ref, held, r.load.at[len(load)])
        load[name].start()
    xall, dyv = r.xall, r.dyv

    lane = lax.broadcasted_iota(jnp.int32, (1, 128), 1)
    low = (lane < 64).astype(F32)
    high = 1.0 - low
    lowb, highb = low.astype(BF), high.astype(BF)
    hm = (lowb, highb)
    first_core = core == 0

    tmp = r.tmp

    def unpack(name, height, width):
        load[name].wait()
        ref = getattr(r, name)
        lines = height * width // 128
        tmp[0:lines, :] = ref[...].astype(F32)
        step = width // 128
        return [tmp[pl.ds(j, height, stride=step), :].astype(BF) for j in range(step)]

    own = (at["a"], at["p"], at["r"], at["i"], core)
    agq, ago, agu, agd = r.agq, r.ago, r.agu, r.agd
    for w, ref in enumerate(("wq", "wk", "wv", "wc")):
        blk = unpack(ref, 16, 512)
        for j in range(2):
            cols = slice(w * 256 + j * 128, w * 256 + j * 128 + 128)
            agq[own + (slice(None), cols)] = jnp.where(first_core, blk[j], blk[2 + j])
            r.sendq[:, cols] = jnp.where(first_core, blk[2 + j], blk[j])
    for ref, buf, height, width in (("wo", ago, 16, 512), ("wu", agu, 16, FF), ("wd", agd, 64, 512)):
        for j, blk in enumerate(unpack(ref, height, width)):
            buf[own + (slice(None), slice(j * 128, j * 128 + 128))] = blk

    norm1 = r.norm1
    mini = r.mini
    mini[core, 0:2, :] = seg_ref[...].astype(F32)
    mini[core, 2:4, :] = pad_ref[...].astype(F32)
    mini[core, 4:8, :] = jnp.zeros((4, 128), F32)

    load["x"].wait()
    pl.semaphore_wait(barrier, len(greet))

    swap_w = remote(r.sendq, agq.at[own], mate)
    swap_m = remote(mini.at[core], mini.at[core], mate)
    swap_n = remote(xall.at[:, core], xall.at[:, core], mate)

    def gather(buf, axis, done, lo, width):
        cols = pl.ds(lo, width)
        index = tuple(slice(None) if d in done else pl.ds(at[d], 1) for d in AXES)
        ref = buf.at[index + (slice(None), cols)]
        return [
            remote(ref, ref, device(**{axis: lax.rem(at[axis] + k, size[axis])}))
            for k in range(1, size[axis])
        ]

    swap_w.wait_recv()
    flying, done = {}, ["c" if part[0] == "agq" else "" for part in GATHER]

    def go_on(n):
        buf, lo, width, order = GATHER[n]
        if n in flying:
            arrived(flying.pop(n))
        left = [d for d in order + "c" if d not in done[n]]
        if left:
            flying[n] = gather(getattr(r, buf), left[0], done[n], lo, width)
            done[n] += left[0]

    sums = []

    agenda = iter(SCHEDULE)

    def point():
        for n in next(agenda):
            if n < len(GATHER):
                go_on(n)
            else:
                sums[n - len(GATHER)].advance()

    point()
    arrived([swap_m, swap_n])
    point()
    unit, inv = norm_rows(xall[...].reshape(512, 512).astype(F32))
    r.unit1[...] = unit.reshape(SEQB, 2, TOK, 512)
    r.inv1[...] = jnp.broadcast_to(inv, (512, 128)).reshape(SEQB, 2, TOK, 128)
    normed = (unit * ga_ref[...]).astype(BF)
    norm1[...] = normed.reshape(SEQB, 2, TOK, 512)
    r.norm1t[...] = normed.T

    turned = [mini[s].T for s in range(2)]
    big_row = lax.broadcasted_iota(jnp.int32, (256, 256), 0)
    big_col = lax.broadcasted_iota(jnp.int32, (256, 256), 1)
    for b in range(SEQB):
        seg_row = jnp.concatenate([mini[0, b : b + 1, :], mini[1, b : b + 1, :]], axis=1)
        seg_col = jnp.concatenate([t[:, b : b + 1] for t in turned], axis=0)
        pad_col = jnp.concatenate([t[:, 2 + b : 3 + b] for t in turned], axis=0)
        same = seg_col == seg_row
        r.mask[b] = jnp.where(same & (big_row >= big_col), 1.0, 0.0)
        r.maskt[b] = jnp.where(same & (big_row <= big_col), 1.0, 0.0)
        seg_last = seg_row[:, 255:256]
        r.last[b] = jnp.broadcast_to((seg_col == seg_last).astype(F32), (256, 128))
        r.padb[b] = jnp.broadcast_to(pad_col, (256, 128))
        r.info[4 + b : 5 + b, :] = jnp.broadcast_to(seg_last, (1, 128))
        r.info[6 + b : 7 + b, :] = jnp.broadcast_to(seg_row[:, 0:1], (1, 128))

    def project(w):
        point()
        mat = agq[..., w * 256 : w * 256 + 256].reshape(512, 256)
        for b in range(SEQB):
            out = nn(norm1[b].reshape(256, 512), mat)
            for pair in range(2):
                part = out[:, pair * 128 : pair * 128 + 128]
                n = b * 2 + pair
                if w == 3:
                    weight = jnp.exp(part) * r.padb[b]
                    r.w[n] = weight
                    r.whi[n], r.wlo[n] = halves(weight)
                else:
                    (r.q, r.k, r.v)[w][n] = part.astype(BF)

    for w in (3, 1, 2):
        project(w)

    def fold(full):
        return full[0:64] * low + full[64:128] * high

    def put_state(ref, n, which, value):
        for t in range(per):
            ref[(n * 2 + which) * per + t, 0:rows, :] = value[t * rows : (t + 1) * rows].astype(ref.dtype)

    def get_block(ref, n, which):
        value = ref[pl.ds((n * 2 + which) * per, per)].astype(F32).reshape(64, 128)
        return jnp.concatenate([value * low, value * high], axis=0)

    def pack_state(key_sum, value_sum):
        return jnp.concatenate([*halves(key_sum), value_sum.astype(BF)], axis=0)

    def carried(n, which):
        value = r.stin[pl.ds(n * share_of, share_of), which * third : (which + 1) * third, :].reshape(64, 128)
        return jnp.concatenate([value * lowb, value * highb], axis=0)

    def local_state(n, carry):
        weight = r.w[n] * r.last[n // 2]
        hi, lo = halves(weight)
        sums_of = [fold(tn(hi, rhs) + tn(lo, rhs)) for rhs in (r.k[n], r.v[n])]
        for part in range(share_of):
            lines = slice(part * third, part * third + third)
            r.sloc[n * share_of + part, 0 : 3 * third, :] = pack_state(*[v[lines] for v in sums_of])
        r.info[pl.ds(n, 1), :] = jnp.sum(weight, axis=0, keepdims=True)
        return carry

    point()
    lax.fori_loop(0, 4, local_state, 0)

    def spread(src, dst, info):
        for t in range(nch):
            src[t, src.shape[1] - 16 :, :] = info
        dst[chip] = src[chip]
        return [
            remote(src.at[lax.rem(chip + k, nch)], dst.at[chip], chip_device(lax.rem(chip + k, nch)))
            for k in range(1, nch)
        ]

    def back(src, dst):
        dst[chip] = src[chip]
        return [
            remote(src.at[lax.rem(chip + k, nch)], dst.at[chip], chip_device(lax.rem(chip + k, nch)))
            for k in range(1, nch)
        ]

    point()
    out_1 = spread(r.sloc, r.rcv, jnp.concatenate(halves(r.info[...]), axis=0))

    project(0)

    def mix_local(n, carry):
        q, k, whi, wlo = r.q[n], r.k[n], r.whi[n], r.wlo[n]
        mask = r.mask[n // 2]
        num = jnp.zeros((256, 128), F32)
        for m in hm:
            hi, lo = halves(nt(q * m, k) * mask)
            num += nn(hi, whi * m) + nn(lo, whi * m) + nn(hi, wlo * m)
        r.num[n] = num
        maskb = mask.astype(BF)
        r.tot[n] = nn(maskb, whi) + nn(maskb, wlo)
        return carry

    point()
    lax.fori_loop(0, 4, mix_local, 0)
    point()

    arrived(out_1)
    point()
    rcv = r.rcv
    owned = (chip * rows) // 256

    def last_of(p, b):
        return r.infos[p, pl.ds(4 + b, 1), :]

    def first_of(p, b):
        return r.infos[p, pl.ds(6 + b, 1), :]

    for p in range(nch):
        lines = rcv[p, 3 * third :, :].astype(F32)
        r.infos[p] = lines[0:8] + lines[8:16]
    run_k = jnp.zeros((third, 128), F32)
    run_v = run_k
    for p in range(nch):
        r.snd[p] = pack_state(run_k, run_v)
        got = rcv[p, 0 : 3 * third, :].astype(F32)
        new_k, new_v = got[0:third] + got[third : 2 * third], got[2 * third :]
        if p == 0:
            run_k, run_v = new_k, new_v
        else:
            keep = (last_of(p - 1, owned) == last_of(p, owned)).astype(F32)
            run_k, run_v = new_k + keep * run_k, new_v + keep * run_v
    point()
    out_2 = back(r.snd, r.stin)
    point()
    zrun = [jnp.zeros((2, 128), F32) for _ in range(SEQB)]
    for p in range(nch - 1):
        for b in range(SEQB):
            z = r.infos[p, 2 * b : 2 * b + 2, :]
            if p > 0:
                z = z + (last_of(p - 1, b) == last_of(p, b)).astype(F32) * zrun[b]
            zrun[b] = jnp.where(p < chip, z, zrun[b])
    before = jnp.maximum(chip - 1, 0)
    for b in range(SEQB):
        r.zin[2 * b : 2 * b + 2, :] = zrun[b]
        open_doc = jnp.where(chip > 0, last_of(before, b), -1.0)[:, 0:1]
        seg_col = jnp.concatenate([t[:, b : b + 1] for t in turned], axis=0)
        r.use[b] = jnp.broadcast_to((seg_col == open_doc).astype(F32), (256, 128))

    point()
    arrived(out_2)

    def both(op, v):
        if op is jnp.max:
            a = jnp.max(jnp.where(lane < 64, v, -jnp.inf), axis=1, keepdims=True)
            b = jnp.max(jnp.where(lane < 64, -jnp.inf, v), axis=1, keepdims=True)
        else:
            a = jnp.sum(v * low, axis=1, keepdims=True)
            b = jnp.sum(v * high, axis=1, keepdims=True)
        return jnp.where(lane < 64, a, b)

    def mix_rest(n, carry):
        b = n // 2
        q, v, whi = r.q[n], r.v[n], r.whi[n]
        mask, use = r.mask[b], r.use[b]
        khi, klo = carried(n, 0), carried(n, 1)
        num = r.num[n] + use * (nt(q, khi) + nt(q, klo))
        tot = r.tot[n] + use * r.zin[pl.ds(n, 1), :]
        floor = jnp.maximum(tot, 1.0)
        score = num / (floor * 8.0)
        e = jnp.exp(score - both(jnp.max, score))
        share = e / (both(jnp.sum, e) * floor)
        r.tot[n] = tot
        r.score[n] = score
        r.share[n] = share
        sb = share.astype(BF)
        out = use * nn(sb, carried(n, 2))
        for m in hm:
            out += nn((nt(sb * m, whi) * mask).astype(BF), v * m)
        r.outb[n] = out.astype(BF).reshape(2, TOK, 128)
        return carry

    point()
    lax.fori_loop(0, 4, mix_rest, 0)
    point()
    swap_o = remote(r.outb.at[:, 1 - core], r.mixx.at[core], mate)
    for n in range(4):
        r.mixx[core, n] = r.outb[n, core]

    point()
    swap_o.wait_recv()
    point()
    mixx = r.mixx
    for b in range(SEQB):
        r.mixed[b * TOK : (b + 1) * TOK, :] = jnp.concatenate(
            [mixx[h, b * 2 + p] for h in range(2) for p in range(2)], axis=1
        )
    w_out = ago[...].reshape(512, 512)
    residual = xall[:, core].reshape(256, 512).astype(F32) + nn(r.mixed[...], w_out)
    r.res[...] = residual
    unit, inv = norm_rows(residual)
    r.unit2[...] = unit
    r.inv2[...] = jnp.broadcast_to(inv, (256, 128))
    r.n2[...] = (unit * gf_ref[...]).astype(BF)
    r.n2t[...] = r.n2[...].T

    class Sum:
        def __init__(self, name, buffer, order, width, height, lo, emit):
            self.emit = emit
            self.name, self.order, self.width, self.height = name, order, width, height
            self.ref, self.lo, self.dims, self.step = getattr(r, buffer), lo, list(AXES), 0
            self.going = False

        def start(self):
            ax = self.order[self.step]
            p = self.dims.index(ax)
            cols = pl.ds(self.lo, self.width)
            land = getattr(r, f"r{self.name}_{self.step}")
            self.copies, self.going = [], True
            for k in range(1, size[ax]):
                to = lax.rem(at[ax] + k, size[ax])
                index = [slice(None)] * len(self.dims) + [slice(None), cols]
                index[p] = to
                self.copies.append(remote(self.ref.at[tuple(index)], land.at[k - 1], device(**{ax: to})))

        def advance(self):
            if self.going:
                self.finish()
            if self.step < len(self.order):
                self.start()

        def finish(self):
            emit = self.emit if self.step == len(self.order) - 1 else None
            ax = self.order[self.step]
            p = self.dims.index(ax)
            arrived(self.copies)
            land = getattr(r, f"r{self.name}_{self.step}")
            cols = slice(self.lo, self.lo + self.width)
            left = [size[d] for d in self.dims if d != ax]
            total = 1
            for extent in left:
                total *= extent
            into = None if emit else getattr(r, f"s{self.name}_{self.step}")

            def one(flat):
                index, rest_of = [], flat
                for extent in reversed(left):
                    index.insert(0, rest_of % extent if isinstance(rest_of, int) else lax.rem(rest_of, extent))
                    rest_of = rest_of // extent
                full = list(index)
                full.insert(p, at[ax])
                value = self.ref[tuple(full) + (slice(None), cols)].astype(F32)
                for k in range(size[ax] - 1):
                    value += land[(k,) + tuple(index)].astype(F32)
                if emit:
                    emit(index, value)
                else:
                    into[tuple(index)] = value.astype(BF)

            if total <= 2:
                for flat in range(total):
                    one(flat)
            else:
                def body(flat, carry):
                    one(flat)
                    return carry

                lax.fori_loop(0, total, body, 0)
            self.dims.remove(ax)
            self.ref, self.lo, self.step = into, 0, self.step + 1

    def to_rows(out_ref, height, width, lo):
        def emit(index, value):
            step = width // 128
            for j in range(value.shape[1] // 128):
                out_ref[pl.ds(lo // 128 + j, height, stride=step), :] = value[:, j * 128 : j * 128 + 128]

        return emit

    shards = {}

    def to_core(name):
        def emit(index, value):
            shards[name, index[0]] = value
            if index[0] == 1:
                at_lo = slice(PIECE[name][2], PIECE[name][2] + 256)
                halves_of = (shards[name, 0], shards[name, 1])
                r.final[core, :, at_lo] = jnp.where(first_core, *halves_of)
                r.fsend[:, at_lo] = jnp.where(first_core, *reversed(halves_of))

        return emit

    outs = dict(go=(oo_ref, 16, 512), gu=(ou_ref, 16, FF), gd=(od_ref, 64, 512))
    for name, (buf, order, lo, width, height) in enumerate(PIECE):
        emit = to_core(name) if buf == "gq" else to_rows(*outs[buf], lo)
        sums.append(Sum(name, buf, order, width, height, lo, emit))

    load["dy"].wait()
    dy = dyv[...].reshape(256, 512)
    blocks = [(j // 2, j % 2) if na == 2 else (0, j // 2, j % 2) for j in range(4)]
    for j in range(4):
        point()
        cols = slice(j * 512, j * 512 + 512)
        pre = nn(r.n2[...], agu[..., cols].reshape(512, 512))
        sig = 1.0 / (1.0 + jnp.exp(-pre))
        hidden = (pre * sig).astype(BF)
        r.hidden[:, cols] = hidden
        r.dsilu[:, cols] = sig * (1.0 + pre * (1.0 - sig))
        r.gd[blocks[j]] = tn(hidden, dy).astype(BF).reshape(lead[len(blocks[j]) :] + (64, 512))
    for j in range(4):
        point()
        cols = slice(j * 512, j * 512 + 512)
        d_pre = (nt(dy, agd[blocks[j]].reshape(512, 512)) * r.dsilu[:, cols]).astype(BF)
        part = nt(d_pre, agu[..., cols].reshape(512, 512))
        r.dn2[...] = part if j == 0 else r.dn2[...] + part
        r.gu[..., cols] = nn(r.n2t[...], d_pre).astype(BF).reshape(lead + (16, 512))
    point()

    dn2 = r.dn2[...]
    unit = r.unit2[...]
    gains2 = jnp.sum(dn2 * unit, axis=0, keepdims=True)
    d_res = dy.astype(F32) + norm_back(
        dn2 * gf_ref[...], unit, r.inv2[:, 0:1]
    )
    r.dres[...] = d_res
    d_attn = d_res.astype(BF)
    d_mixed = nt(d_attn, w_out).astype(BF)
    for b in range(SEQB):
        for p in range(2):
            part = [d_mixed[b * TOK : (b + 1) * TOK, h * 256 + p * 128 : h * 256 + p * 128 + 128] for h in range(2)]
            r.do[b * 2 + p, core] = jnp.where(first_core, part[0], part[1])
            r.senddo[b * 2 + p] = jnp.where(first_core, part[1], part[0])
    point()
    swap_d = remote(r.senddo, r.do.at[:, core], mate)
    point()
    swap_d.wait_recv()

    def mix_back(n, carry):
        b = n // 2
        q, v, whi = r.q[n], r.v[n], r.whi[n]
        mask, use = r.mask[b], r.use[b]
        share, tot, score = r.share[n], r.tot[n], r.score[n]
        d_out = r.do[n].reshape(256, 128)
        ds = use * nt(d_out, carried(n, 2))
        for m in hm:
            ds += nn((nt(d_out * m, v) * mask).astype(BF), whi * m)
        floor = jnp.maximum(tot, 1.0)
        inv_floor = 1.0 / floor
        prob = share * floor
        dprob = ds * inv_floor
        dscore = prob * (dprob - both(jnp.sum, dprob * prob))
        dnum = dscore * inv_floor * 0.125
        gate = jnp.where(tot > 1.0, 1.0, jnp.where(tot == 1.0, 0.5, 0.0))
        dtot = -(ds * share + dscore * score) * inv_floor * gate
        r.dnum[n] = dnum.astype(BF)
        r.dtot[n] = dtot
        put_state(r.dloc, n, 0, fold(tn((use * dnum).astype(BF), q)))
        put_state(r.dloc, n, 1, fold(tn((use * share).astype(BF), d_out)))
        r.gz[pl.ds(n, 1), :] = jnp.sum(use * dtot, axis=0, keepdims=True)
        return carry

    point()
    lax.fori_loop(0, 4, mix_back, 0)
    point()
    r.gz[4:8, :] = jnp.zeros((4, 128), F32)
    gz_parts = jnp.concatenate(halves(r.gz[...]), axis=0)
    out_3 = spread(r.dloc, r.drcv, gz_parts)

    def mix_back_local(n, carry):
        b = n // 2
        q, k, v, whi, w = r.q[n], r.k[n], r.v[n], r.whi[n], r.w[n]
        mask, maskt, use = r.mask[b], r.maskt[b], r.use[b]
        d_out, dnum = r.do[n].reshape(256, 128), r.dnum[n]
        sb = r.share[n].astype(BF)
        dq = use * nn(dnum, carried(n, 0))
        dk = jnp.zeros((256, 128), F32)
        dv = jnp.zeros((256, 128), F32)
        dw = nn(maskt.astype(BF), r.dtot[n].astype(BF))
        for m in hm:
            dq += nn((nt(dnum * m, whi) * mask).astype(BF), k * m)
            dk += nn((nt(whi * m, dnum) * maskt).astype(BF), q * m)
            dv += nn((nt(whi * m, sb) * maskt).astype(BF), d_out * m)
            dw += nn((nt(v * m, d_out) * maskt).astype(BF), sb * m)
            dw += nn((nt(k * m, q) * maskt).astype(BF), dnum * m)
        cols = pl.ds(pl.multiple_of(lax.rem(n, 2) * 128, 128), 128)
        r.dd[b, :, :, cols] = dq.astype(BF).reshape(2, TOK, 128)
        r.dkl[n] = dk
        r.dvl[n] = dv
        r.dwl[n] = dw
        return carry

    point()
    lax.fori_loop(0, 4, mix_back_local, 0)
    dd = r.dd

    def weight_gradient(lo, width):
        value = nn(r.norm1t[...], dd[:, :, :, lo : lo + width].reshape(512, width))
        r.gq[..., lo : lo + width] = value.astype(BF).reshape(lead + (16, width))

    point()

    arrived(out_3)
    point()
    drcv = r.drcv
    run = jnp.zeros((rows, 128), F32)
    for p in reversed(range(nch)):
        r.dsnd[p] = run.astype(BF)
        here = drcv[p, 0:rows, :].astype(F32)
        if p == nch - 1:
            run = here
        else:
            run = here + (first_of(p, owned) == first_of(p + 1, owned)).astype(F32) * run
    point()
    out_4 = back(r.dsnd, r.gin)
    point()
    zrun = [jnp.zeros((2, 128), F32) for _ in range(SEQB)]
    for p in reversed(range(1, nch)):
        for b in range(SEQB):
            tail = drcv[p, rows : rows + 16, :].astype(F32)
            z = tail[2 * b : 2 * b + 2] + tail[8 + 2 * b : 10 + 2 * b]
            if p < nch - 1:
                z = z + (first_of(p, b) == first_of(p + 1, b)).astype(F32) * zrun[b]
            zrun[b] = jnp.where(p > chip, z, zrun[b])
    after = jnp.minimum(chip + 1, nch - 1)
    for b in range(SEQB):
        r.gz[2 * b : 2 * b + 2, :] = zrun[b]
        matched = (first_of(after, b) == r.info[4 + b : 5 + b, :]) & (chip < nch - 1)
        r.last[b] = r.last[b] * matched.astype(F32)
    point()
    r.go[...] = tn(r.mixed[...], d_attn).astype(BF).reshape(lead + (16, 512))
    point()
    y_rows = r.res[...] + nn(r.hidden[...], agd[...].reshape(FF, 512))
    y_ref[...] = y_rows.astype(BF).reshape(SEQB, TOK, 512)

    point()
    weight_gradient(0, 256)
    point()
    arrived(out_4)

    def mix_last(slot, value):
        def one(n, carry):
            cols = pl.ds(pl.multiple_of(slot * 256 + lax.rem(n, 2) * 128, 128), 128)
            dd[n // 2, :, :, cols] = value(n, r.last[n // 2]).astype(BF).reshape(2, TOK, 128)
            return carry

        point()
        lax.fori_loop(0, 4, one, 0)
        point()
        weight_gradient(slot * 256, 256)

    def state_gradient(n, which):
        return get_block(r.gin, n, which).astype(BF)

    def weight_value(n, last):
        more = nt(r.k[n], state_gradient(n, 0)) + nt(r.v[n], state_gradient(n, 1)) + r.gz[pl.ds(n, 1), :]
        return (r.dwl[n] + last * more) * r.w[n]

    mix_last(2, lambda n, last: r.dvl[n] + last * nn(r.whi[n], state_gradient(n, 1)))
    mix_last(1, lambda n, last: r.dkl[n] + last * nn(r.whi[n], state_gradient(n, 0)))
    mix_last(3, weight_value)

    point()
    full_q = agq[...].reshape(512, 1024)
    gains1 = jnp.zeros((1, 512), F32)
    for b in range(SEQB):
        part = nt(dd[b].reshape(256, 1024), full_q)
        r.dn1[:, b] = part.reshape(2, TOK, 512)
        gains1 += jnp.sum(part * r.unit1[b].reshape(256, 512), axis=0, keepdims=True)
    point()
    swap_g = remote(r.dn1.at[1 - core], r.dn1r, mate)

    gains = jnp.concatenate(
        [g[:, j * 128 : j * 128 + 128] for g in (gains1, gains2) for j in range(4)], axis=0
    )

    def exchange(buf, value, me, count, dev):
        buf[me] = value
        return [remote(buf.at[me], buf.at[me], dev(lax.rem(me + k, count))) for k in range(1, count)]

    def total(buf, copies, count):
        arrived(copies)
        value = buf[0]
        for k in range(1, count):
            value = value + buf[k]
        return value

    point()
    copies = exchange(r.gain1, gains, core, 2, lambda t: device(c=t))

    point()
    swap_g.wait_recv()
    point()
    dn1 = (r.dn1[core] + r.dn1r[...]).reshape(256, 512)
    unit = r.unit1[:, core].reshape(256, 512)
    dx = r.dres[...] + norm_back(dn1 * ga_ref[...], unit, r.inv1[:, core].reshape(256, 128)[:, 0:1])
    dx_ref[...] = dx.astype(BF).reshape(SEQB, TOK, 512)

    point()
    gains = total(r.gain1, copies, 2)
    point()
    copies = exchange(r.gain2, gains, chip, nch, chip_device)
    point()
    gains = total(r.gain2, copies, nch)
    point()
    copies = exchange(r.gain3, gains, at["a"], na, lambda t: device(a=t))

    final = r.final
    point()
    swap_f = remote(r.fsend, final.at[core], mate)
    point()
    gains = total(r.gain3, copies, na)
    for ref, first in ((og1_ref, 0), (og2_ref, 4)):
        for j in range(4):
            ref[:, j * 128 : j * 128 + 128] = gains[first + j : first + j + 1]
    point()
    swap_f.wait_recv()
    for ref, lo in ((oq_ref, 0), (ok_ref, 256), (ov_ref, 512), (oc_ref, 768)):
        for j in range(4):
            ref[pl.ds(j, 16, stride=4), :] = final[j // 2, :, lo + (j % 2) * 128 : lo + (j % 2) * 128 + 128]
    point()
    for copy in started:
        copy.wait_send()


def hand_over(count, *refs):
    src, dst, held, sems = refs[:count], refs[count : 2 * count], refs[2 * count : 3 * count], refs[3 * count]
    into = [pltpu.make_async_copy(src[n], held[n], sems.at[0, n]) for n in range(count)]
    away = [pltpu.make_async_copy(held[n], dst[n], sems.at[1, n]) for n in range(count)]
    for copy in into:
        copy.start()
    for n in range(count):
        into[n].wait()
        away[n].start()
    for copy in away:
        copy.wait()


def solution(mesh):
    ndp, nseq = mesh.shape["dp"], mesh.shape["seq"]
    joint = D // (ndp * nseq) >= 16
    na = ndp if joint else 1
    ni = nseq // (2 * OUTER)
    scratch = layout(na, ni)
    names = tuple(scratch)
    both_axes = ("dp", "seq")

    def body(x, dy, seg, pad, *args):
        weights, (gain_attn, gain_ffn) = args[:7], args[7:]
        shards = []
        for w in weights:
            if not joint:
                whole = lax.all_gather(w, both_axes, axis=0, tiled=True).reshape(nseq, -1)
                w = lax.dynamic_index_in_dim(whole, lax.axis_index("seq"), 0, keepdims=False)
            shards.append(w.reshape(-1, 128))
        outs = [jax.ShapeDtypeStruct(x.shape, BF)] * 2
        outs += [jax.ShapeDtypeStruct(w.shape, F32) for w in shards]
        outs += [jax.ShapeDtypeStruct((1, D), F32)] * 2
        vmem, hbm = pl.BlockSpec(memory_space=pltpu.VMEM), pl.BlockSpec(memory_space=pltpu.HBM)
        got = pl.pallas_call(
            functools.partial(kernel, na, ni, names),
            out_shape=outs,
            in_specs=[hbm] * 2 + [vmem] * 2 + [hbm] * 7 + [vmem] * 2,
            out_specs=[vmem] * 11,
            scratch_shapes=list(scratch.values()),
            compiler_params=pltpu.CompilerParams(
                collective_id=0, has_side_effects=True, vmem_limit_bytes=62 * 2**20
            ),
            cost_estimate=pl.CostEstimate(flops=12 * 10**9, bytes_accessed=4 * 2**20, transcendentals=10**6),
            name="block",
        )(x, dy, seg, pad, *shards, gain_attn.reshape(1, D), gain_ffn.reshape(1, D))
        got = pl.pallas_call(
            functools.partial(hand_over, 11),
            out_shape=outs,
            in_specs=[hbm] * 11,
            out_specs=[hbm] * 11,
            scratch_shapes=[pltpu.VMEM(o.shape, o.dtype) for o in outs] + [pltpu.SemaphoreType.DMA((2, 11))],
            name="results",
        )(*got)
        y, dx = got[:2]
        grads = [g.reshape(-1) for g in got[2:9]]
        gains = [g.reshape(-1) for g in got[9:]]
        if not joint:
            index = lax.axis_index("dp") * nseq + lax.axis_index("seq")
            grads = [lax.psum(g, "dp") for g in grads]
            grads = [lax.all_gather(g, "seq", axis=0, tiled=True) for g in grads]
            grads = [
                lax.dynamic_slice_in_dim(g, index * (g.shape[0] // (ndp * nseq)), g.shape[0] // (ndp * nseq))
                for g in grads
            ]
            gains = [lax.psum(g, "dp") for g in gains]
        return (y, dx, *grads, *gains)

    data, ids, flat = P("dp", "seq", None), P("dp", "seq"), P(("dp", "seq"))
    return jax.shard_map(
        body,
        mesh=mesh,
        in_specs=(data, data, ids, ids) + (flat,) * 7 + (P(), P()),
        out_specs=(data, data) + (flat,) * 7 + (P(), P()),
        check_vma=False,
    )
```

```python
import functools
import types

import jax
import jax.numpy as jnp
from jax import lax
from jax.experimental import pallas as pl
from jax.experimental.pallas import tpu as pltpu
from jax.sharding import PartitionSpec as P

D = 512
FF = 2048
TOK = 128
SEQB = 2
OUTER = 4
BF = jnp.bfloat16
F32 = jnp.float32
EPS = 1e-05
MESH = pl.DeviceIdType.MESH
AXES = "apric"


GATHER = (
    ("agq", 768, 256, "rpia"),
    ("agq", 256, 256, "pari"),
    ("agq", 512, 256, "rpia"),
    ("agq", 0, 256, "apri"),
    ("ago", 0, 512, "piar"),
    ("agu", 0, 512, "pira"),
    ("agu", 512, 512, "rpai"),
    ("agu", 1024, 512, "iapr"),
    ("agu", 1536, 512, "ipar"),
    ("agd", 0, 128, "pria"),
    ("agd", 128, 128, "rpai"),
    ("agd", 256, 128, "prai"),
    ("agd", 384, 128, "prai"),
)
PIECE = (
    ("gq", "iarp", 0, 256, 16),
    ("gq", "airp", 256, 256, 16),
    ("gq", "iarp", 512, 256, 16),
    ("gq", "raip", 768, 256, 16),
    ("go", "cripa", 0, 512, 16),
    ("gu", "cripa", 0, 512, 16),
    ("gu", "ciarp", 512, 512, 16),
    ("gu", "capri", 1024, 512, 16),
    ("gu", "ciapr", 1536, 512, 16),
    ("gd", "cairp", 0, 128, 64),
    ("gd", "crapi", 128, 128, 64),
    ("gd", "cripa", 256, 128, 64),
    ("gd", "caipr", 384, 128, 64),
)
SCHEDULE = (
    (0, 11, 9),
    (7, 2, 1),
    (4, 0, 11, 3, 12, 9, 6, 1, 2, 7, 3, 0, 11, 10, 9, 1, 2, 10, 0, 8, 4, 5, 3, 1, 7, 6, 2, 12, 10, 3, 8, 5, 7, 0, 4),
    (11, 1),
    (6, 2),
    (),
    (),
    (9, 7, 12, 3, 4, 5, 10, 8),
    (),
    (11,),
    (),
    (),
    (9, 5, 6, 4, 7, 9),
    (10, 4, 8, 10, 12),
    (),
    (),
    (6, 11, 5, 8, 12),
    (),
    (6, 5),
    (),
    (12,),
    (8,),
    (24,),
    (25,),
    (),
    (20,),
    (21,),
    (),
    (25, 23, 20, 24, 21),
    (),
    (),
    (18, 23),
    (),
    (),
    (),
    (),
    (24,),
    (18, 23, 19),
    (),
    (13, 22, 21, 20),
    (25, 17),
    (22, 24),
    (15,),
    (21, 17),
    (),
    (19, 14),
    (20, 16, 18),
    (13, 15),
    (25, 17, 14),
    (21, 19, 23),
    (),
    (),
    (),
    (24, 15, 16, 22, 13, 18, 17, 20, 14),
    (19, 15, 16, 13, 22, 14, 25, 18),
    (19, 16, 24, 22, 15, 17, 23, 21, 14, 13, 20, 16),
    (19, 17, 23, 25, 18),
    (),
    (22,),
)


def nn(a, b):
    return jnp.dot(a, b, preferred_element_type=F32)


def nt(a, b):
    return lax.dot_general(a, b, (((1,), (1,)), ((), ())), preferred_element_type=F32)


def tn(a, b):
    return lax.dot_general(a, b, (((0,), (0,)), ((), ())), preferred_element_type=F32)


def halves(v):
    high = v.astype(BF)
    return high, (v - high.astype(F32)).astype(BF)


def norm_rows(v):
    center = v - jnp.mean(v, axis=-1, keepdims=True)
    inv = lax.rsqrt(jnp.mean(center * center, axis=-1, keepdims=True) + EPS)
    return center * inv, inv


def norm_back(g, unit, inv):
    return inv * (
        g - jnp.mean(g, axis=-1, keepdims=True) - unit * jnp.mean(g * unit, axis=-1, keepdims=True)
    )


def layout(na, ni):
    nch = OUTER * ni
    rows = 512 // nch
    lead = (na, 2, 2, ni, 2)
    s = {}

    def vm(name, shape, dtype):
        s[name] = pltpu.VMEM(tuple(shape), dtype)

    vm("tmp", (256, 128), F32)
    vm("agq", lead + (16, 1024), BF)
    vm("sendq", (16, 1024), BF)
    vm("ago", lead + (16, 512), BF)
    vm("agu", lead + (16, FF), BF)
    vm("agd", lead + (64, 512), BF)
    vm("unit1", (SEQB, 2, TOK, 512), F32)
    vm("inv1", (SEQB, 2, TOK, 128), F32)
    vm("norm1", (SEQB, 2, TOK, 512), BF)
    vm("mini", (2, 8, 128), F32)
    for m in ("mask", "maskt"):
        vm(m, (SEQB, 256, 256), F32)
    for m in ("last", "use", "padb"):
        vm(m, (SEQB, 256, 128), F32)
    for m in ("q", "k", "v", "whi", "wlo"):
        vm(m, (4, 256, 128), BF)
    for m in ("w", "num", "tot", "share", "score", "dtot", "dkl", "dvl", "dwl"):
        vm(m, (4, 256, 128), F32)
    vm("dnum", (4, 256, 128), BF)
    vm("info", (8, 128), F32)
    for m, kind, extra in (("dloc", BF, 16), ("drcv", BF, 16)):
        vm(m, (nch, rows + extra, 128), kind)
    for m in ("dsnd", "gin"):
        vm(m, (nch, rows, 128), BF)
    third = 256 // nch
    for m, extra in (("sloc", 16), ("rcv", 16), ("snd", 0), ("stin", 0)):
        vm(m, (nch, 3 * third + extra, 128), BF)
    vm("infos", (nch, 8, 128), F32)
    vm("zin", (8, 128), F32)
    vm("gz", (8, 128), F32)
    vm("outb", (4, 2, TOK, 128), BF)
    vm("mixx", (2, 4, TOK, 128), BF)
    vm("mixed", (256, 512), BF)
    for m in ("res", "unit2", "dn2", "dres"):
        vm(m, (256, 512), F32)
    vm("inv2", (256, 128), F32)
    vm("n2", (256, 512), BF)
    vm("n2t", (512, 256), BF)
    vm("norm1t", (512, 512), BF)
    vm("hidden", (256, FF), BF)
    vm("dsilu", (256, FF), F32)
    vm("xall", (SEQB, 2, TOK, 512), BF)
    vm("dyv", (SEQB, TOK, 512), BF)
    for name, lines in (("wq", 64), ("wk", 64), ("wv", 64), ("wc", 64), ("wo", 64), ("wu", 256), ("wd", 256)):
        vm(name, (lines, 128), BF)
    vm("do", (4, 2, TOK, 128), BF)
    vm("senddo", (4, TOK, 128), BF)
    vm("dd", (SEQB, 2, TOK, 1024), BF)
    vm("dn1", (2, SEQB, TOK, 512), F32)
    vm("dn1r", (SEQB, TOK, 512), F32)
    vm("gq", lead + (16, 1024), BF)
    vm("go", lead + (16, 512), BF)
    vm("gu", lead + (16, FF), BF)
    vm("gd", lead + (64, 512), BF)
    vm("final", (2, 16, 1024), F32)
    vm("fsend", (16, 1024), F32)
    for name, size in (("gain1", 2), ("gain2", nch), ("gain3", na)):
        vm(name, (size, 8, 128), F32)
    for name, (_, order, _, width, height) in enumerate(PIECE):
        dims = list(AXES)
        for step, ax in enumerate(order):
            size = dict(a=na, p=2, r=2, i=ni, c=2)
            dims.remove(ax)
            left = tuple(size[d] for d in dims)
            vm(f"r{name}_{step}", (max(size[ax] - 1, 1),) + left + (height, width), BF)
            if step < len(order) - 1:
                vm(f"s{name}_{step}", left + (height, width), BF)
    s["load"] = pltpu.SemaphoreType.DMA((9,))
    s["sems"] = pltpu.SemaphoreType.DMA((2 * 200,))
    return s


def kernel(na, ni, names, *refs):
    (x_ref, dy_ref, seg_ref, pad_ref, wq_ref, wk_ref, wv_ref, wc_ref, wo_ref, wu_ref, wd_ref) = refs[:11]
    ga_ref, gf_ref = refs[11:13]
    (y_ref, dx_ref, oq_ref, ok_ref, ov_ref, oc_ref, oo_ref, ou_ref, od_ref, og1_ref, og2_ref) = refs[13:24]
    r = types.SimpleNamespace(**dict(zip(names, refs[24:], strict=True)))
    nch = OUTER * ni
    rows = 512 // nch
    per = 64 // rows
    third = 256 // nch
    share_of = 64 // third

    dp = lax.axis_index("dp")
    seq = lax.axis_index("seq")
    chip = seq // 2
    at = dict(
        a=dp if na > 1 else 0,
        p=chip // (2 * ni),
        r=lax.rem(chip // ni, 2),
        i=lax.rem(chip, ni),
        c=lax.rem(seq, 2),
    )
    size = dict(a=na, p=2, r=2, i=ni, c=2)
    lead = (na, 2, 2, ni, 2)
    core = at["c"]

    def device(**moved):
        p = {**at, **moved}
        return (p["a"] if na > 1 else dp, ((p["p"] * 2 + p["r"]) * ni + p["i"]) * 2 + p["c"])

    def chip_device(t):
        return (dp, t * 2 + core)

    started = []
    sems = r.sems

    def remote(src, dst, dev):
        n = len(started)
        copy = pltpu.make_async_remote_copy(
            src_ref=src,
            dst_ref=dst,
            send_sem=sems.at[2 * n],
            recv_sem=sems.at[2 * n + 1],
            device_id=dev,
            device_id_type=MESH,
        )
        copy.start()
        started.append(copy)
        return copy

    def arrived(copies):
        for copy in copies:
            copy.wait_recv()

    sent = [0]

    def drain(count):
        for copy in started[sent[0] : count]:
            copy.wait_send()
        sent[0] = count

    mate = device(c=1 - core)

    barrier = pltpu.get_barrier_semaphore()
    greet = [mate] + [chip_device(lax.rem(chip + k, nch)) for k in range(1, nch)]
    greet += [device(a=lax.rem(at["a"] + k, na)) for k in range(1, na)]
    for dev in greet:
        pl.semaphore_signal(barrier, inc=1, device_id=dev, device_id_type=MESH)

    load = {}
    for name, ref in (
        ("wq", wq_ref), ("wk", wk_ref), ("wv", wv_ref), ("wc", wc_ref), ("x", x_ref),
        ("wo", wo_ref), ("wu", wu_ref), ("wd", wd_ref), ("dy", dy_ref),
    ):
        held = r.xall.at[:, core] if name == "x" else r.dyv if name == "dy" else getattr(r, name)
        load[name] = pltpu.make_async_copy(ref, held, r.load.at[len(load)])
        load[name].start()
    xall, dyv = r.xall, r.dyv

    lane = lax.broadcasted_iota(jnp.int32, (1, 128), 1)
    low = (lane < 64).astype(F32)
    high = 1.0 - low
    lowb, highb = low.astype(BF), high.astype(BF)
    hm = (lowb, highb)
    first_core = core == 0

    tmp = r.tmp

    def unpack(name, height, width):
        load[name].wait()
        ref = getattr(r, name)
        lines = height * width // 128
        tmp[0:lines, :] = ref[...].astype(F32)
        step = width // 128
        return [tmp[pl.ds(j, height, stride=step), :].astype(BF) for j in range(step)]

    own = (at["a"], at["p"], at["r"], at["i"], core)
    agq, ago, agu, agd = r.agq, r.ago, r.agu, r.agd
    for w, ref in enumerate(("wq", "wk", "wv", "wc")):
        blk = unpack(ref, 16, 512)
        for j in range(2):
            cols = slice(w * 256 + j * 128, w * 256 + j * 128 + 128)
            agq[own + (slice(None), cols)] = jnp.where(first_core, blk[j], blk[2 + j])
            r.sendq[:, cols] = jnp.where(first_core, blk[2 + j], blk[j])
    norm1 = r.norm1
    mini = r.mini
    mini[core, 0:2, :] = seg_ref[...].astype(F32)
    mini[core, 2:4, :] = pad_ref[...].astype(F32)
    mini[core, 4:8, :] = jnp.zeros((4, 128), F32)

    load["x"].wait()
    pl.semaphore_wait(barrier, len(greet))

    swap_w = remote(r.sendq, agq.at[own], mate)
    swap_m = remote(mini.at[core], mini.at[core], mate)
    swap_n = remote(xall.at[:, core], xall.at[:, core], mate)

    def gather(buf, axis, done, lo, width):
        cols = pl.ds(lo, width)
        index = tuple(slice(None) if d in done else pl.ds(at[d], 1) for d in AXES)
        ref = buf.at[index + (slice(None), cols)]
        return [
            remote(ref, ref, device(**{axis: lax.rem(at[axis] + k, size[axis])}))
            for k in range(1, size[axis])
        ]

    for ref, buf, height, width in (("wo", ago, 16, 512), ("wu", agu, 16, FF), ("wd", agd, 64, 512)):
        for j, blk in enumerate(unpack(ref, height, width)):
            buf[own + (slice(None), slice(j * 128, j * 128 + 128))] = blk

    swap_w.wait_recv()
    flying, done = {}, ["c" if part[0] == "agq" else "" for part in GATHER]

    def go_on(n):
        buf, lo, width, order = GATHER[n]
        if n in flying:
            arrived(flying.pop(n))
        left = [d for d in order + "c" if d not in done[n]]
        if left:
            flying[n] = gather(getattr(r, buf), left[0], done[n], lo, width)
            done[n] += left[0]

    sums = []

    agenda = iter(SCHEDULE)

    def point():
        for n in next(agenda):
            if n < len(GATHER):
                go_on(n)
            else:
                sums[n - len(GATHER)].advance()

    point()
    arrived([swap_m, swap_n])
    point()
    unit, inv = norm_rows(xall[...].reshape(512, 512).astype(F32))
    r.unit1[...] = unit.reshape(SEQB, 2, TOK, 512)
    r.inv1[...] = jnp.broadcast_to(inv, (512, 128)).reshape(SEQB, 2, TOK, 128)
    normed = (unit * ga_ref[...]).astype(BF)
    norm1[...] = normed.reshape(SEQB, 2, TOK, 512)
    r.norm1t[...] = normed.T

    turned = [mini[s].T for s in range(2)]
    big_row = lax.broadcasted_iota(jnp.int32, (256, 256), 0)
    big_col = lax.broadcasted_iota(jnp.int32, (256, 256), 1)
    for b in range(SEQB):
        seg_row = jnp.concatenate([mini[0, b : b + 1, :], mini[1, b : b + 1, :]], axis=1)
        seg_col = jnp.concatenate([t[:, b : b + 1] for t in turned], axis=0)
        pad_col = jnp.concatenate([t[:, 2 + b : 3 + b] for t in turned], axis=0)
        same = seg_col == seg_row
        r.mask[b] = jnp.where(same & (big_row >= big_col), 1.0, 0.0)
        r.maskt[b] = jnp.where(same & (big_row <= big_col), 1.0, 0.0)
        seg_last = seg_row[:, 255:256]
        r.last[b] = jnp.broadcast_to((seg_col == seg_last).astype(F32), (256, 128))
        r.padb[b] = jnp.broadcast_to(pad_col, (256, 128))
        r.info[4 + b : 5 + b, :] = jnp.broadcast_to(seg_last, (1, 128))
        r.info[6 + b : 7 + b, :] = jnp.broadcast_to(seg_row[:, 0:1], (1, 128))

    def project(w):
        point()
        mat = agq[..., w * 256 : w * 256 + 256].reshape(512, 256)
        for b in range(SEQB):
            out = nn(norm1[b].reshape(256, 512), mat)
            for pair in range(2):
                part = out[:, pair * 128 : pair * 128 + 128]
                n = b * 2 + pair
                if w == 3:
                    weight = jnp.exp(part) * r.padb[b]
                    r.w[n] = weight
                    r.whi[n], r.wlo[n] = halves(weight)
                else:
                    (r.q, r.k, r.v)[w][n] = part.astype(BF)

    for w in (3, 1, 2):
        project(w)

    def fold(full):
        return full[0:64] * low + full[64:128] * high

    def put_state(ref, n, which, value):
        for t in range(per):
            ref[(n * 2 + which) * per + t, 0:rows, :] = value[t * rows : (t + 1) * rows].astype(ref.dtype)

    def get_block(ref, n, which):
        value = ref[pl.ds((n * 2 + which) * per, per)].astype(F32).reshape(64, 128)
        return jnp.concatenate([value * low, value * high], axis=0)

    def pack_state(key_sum, value_sum):
        return jnp.concatenate([*halves(key_sum), value_sum.astype(BF)], axis=0)

    def carried(n, which):
        value = r.stin[pl.ds(n * share_of, share_of), which * third : (which + 1) * third, :].reshape(64, 128)
        return jnp.concatenate([value * lowb, value * highb], axis=0)

    def local_state(n, carry):
        weight = r.w[n] * r.last[n // 2]
        hi, lo = halves(weight)
        sums_of = [fold(tn(hi, rhs) + tn(lo, rhs)) for rhs in (r.k[n], r.v[n])]
        for part in range(share_of):
            lines = slice(part * third, part * third + third)
            r.sloc[n * share_of + part, 0 : 3 * third, :] = pack_state(*[v[lines] for v in sums_of])
        r.info[pl.ds(n, 1), :] = jnp.sum(weight, axis=0, keepdims=True)
        return carry

    point()
    lax.fori_loop(0, 4, local_state, 0)

    def spread(src, dst, info):
        for t in range(nch):
            src[t, src.shape[1] - 16 :, :] = info
        dst[chip] = src[chip]
        return [
            remote(src.at[lax.rem(chip + k, nch)], dst.at[chip], chip_device(lax.rem(chip + k, nch)))
            for k in range(1, nch)
        ]

    def back(src, dst):
        dst[chip] = src[chip]
        return [
            remote(src.at[lax.rem(chip + k, nch)], dst.at[chip], chip_device(lax.rem(chip + k, nch)))
            for k in range(1, nch)
        ]

    point()
    mark = len(started)
    out_1 = spread(r.sloc, r.rcv, jnp.concatenate(halves(r.info[...]), axis=0))

    project(0)

    def mix_local(n, carry):
        q, k, whi, wlo = r.q[n], r.k[n], r.whi[n], r.wlo[n]
        mask = r.mask[n // 2]
        num = jnp.zeros((256, 128), F32)
        for m in hm:
            hi, lo = halves(nt(q * m, k) * mask)
            num += nn(hi, whi * m) + nn(lo, whi * m) + nn(hi, wlo * m)
        r.num[n] = num
        maskb = mask.astype(BF)
        r.tot[n] = nn(maskb, whi) + nn(maskb, wlo)
        return carry

    point()
    lax.fori_loop(0, 4, mix_local, 0)
    point()

    arrived(out_1)
    point()
    rcv = r.rcv
    owned = (chip * rows) // 256

    def last_of(p, b):
        return r.infos[p, pl.ds(4 + b, 1), :]

    def first_of(p, b):
        return r.infos[p, pl.ds(6 + b, 1), :]

    for p in range(nch):
        lines = rcv[p, 3 * third :, :].astype(F32)
        r.infos[p] = lines[0:8] + lines[8:16]
    run_k = jnp.zeros((third, 128), F32)
    run_v = run_k
    for p in range(nch):
        r.snd[p] = pack_state(run_k, run_v)
        got = rcv[p, 0 : 3 * third, :].astype(F32)
        new_k, new_v = got[0:third] + got[third : 2 * third], got[2 * third :]
        if p == 0:
            run_k, run_v = new_k, new_v
        else:
            keep = (last_of(p - 1, owned) == last_of(p, owned)).astype(F32)
            run_k, run_v = new_k + keep * run_k, new_v + keep * run_v
    point()
    out_2 = back(r.snd, r.stin)
    point()
    zrun = [jnp.zeros((2, 128), F32) for _ in range(SEQB)]
    for p in range(nch - 1):
        for b in range(SEQB):
            z = r.infos[p, 2 * b : 2 * b + 2, :]
            if p > 0:
                z = z + (last_of(p - 1, b) == last_of(p, b)).astype(F32) * zrun[b]
            zrun[b] = jnp.where(p < chip, z, zrun[b])
    before = jnp.maximum(chip - 1, 0)
    for b in range(SEQB):
        r.zin[2 * b : 2 * b + 2, :] = zrun[b]
        open_doc = jnp.where(chip > 0, last_of(before, b), -1.0)[:, 0:1]
        seg_col = jnp.concatenate([t[:, b : b + 1] for t in turned], axis=0)
        r.use[b] = jnp.broadcast_to((seg_col == open_doc).astype(F32), (256, 128))

    point()
    drain(mark)
    arrived(out_2)

    def both(op, v):
        if op is jnp.max:
            a = jnp.max(jnp.where(lane < 64, v, -jnp.inf), axis=1, keepdims=True)
            b = jnp.max(jnp.where(lane < 64, -jnp.inf, v), axis=1, keepdims=True)
        else:
            a = jnp.sum(v * low, axis=1, keepdims=True)
            b = jnp.sum(v * high, axis=1, keepdims=True)
        return jnp.where(lane < 64, a, b)

    def mix_rest(n, carry):
        b = n // 2
        q, v, whi = r.q[n], r.v[n], r.whi[n]
        mask, use = r.mask[b], r.use[b]
        khi, klo = carried(n, 0), carried(n, 1)
        num = r.num[n] + use * (nt(q, khi) + nt(q, klo))
        tot = r.tot[n] + use * r.zin[pl.ds(n, 1), :]
        floor = jnp.maximum(tot, 1.0)
        score = num / (floor * 8.0)
        e = jnp.exp(score - both(jnp.max, score))
        share = e / (both(jnp.sum, e) * floor)
        r.tot[n] = tot
        r.score[n] = score
        r.share[n] = share
        sb = share.astype(BF)
        out = use * nn(sb, carried(n, 2))
        for m in hm:
            out += nn((nt(sb * m, whi) * mask).astype(BF), v * m)
        r.outb[n] = out.astype(BF).reshape(2, TOK, 128)
        return carry

    point()
    lax.fori_loop(0, 4, mix_rest, 0)
    point()
    swap_o = remote(r.outb.at[:, 1 - core], r.mixx.at[core], mate)
    for n in range(4):
        r.mixx[core, n] = r.outb[n, core]

    point()
    swap_o.wait_recv()
    point()
    mixx = r.mixx
    for b in range(SEQB):
        r.mixed[b * TOK : (b + 1) * TOK, :] = jnp.concatenate(
            [mixx[h, b * 2 + p] for h in range(2) for p in range(2)], axis=1
        )
    w_out = ago[...].reshape(512, 512)
    residual = xall[:, core].reshape(256, 512).astype(F32) + nn(r.mixed[...], w_out)
    r.res[...] = residual
    unit, inv = norm_rows(residual)
    r.unit2[...] = unit
    r.inv2[...] = jnp.broadcast_to(inv, (256, 128))
    r.n2[...] = (unit * gf_ref[...]).astype(BF)
    r.n2t[...] = r.n2[...].T

    class Sum:
        def __init__(self, name, buffer, order, width, height, lo, emit):
            self.emit = emit
            self.name, self.order, self.width, self.height = name, order, width, height
            self.ref, self.lo, self.dims, self.step = getattr(r, buffer), lo, list(AXES), 0
            self.going = False

        def start(self):
            ax = self.order[self.step]
            p = self.dims.index(ax)
            cols = pl.ds(self.lo, self.width)
            land = getattr(r, f"r{self.name}_{self.step}")
            self.copies, self.going = [], True
            for k in range(1, size[ax]):
                to = lax.rem(at[ax] + k, size[ax])
                index = [slice(None)] * len(self.dims) + [slice(None), cols]
                index[p] = to
                self.copies.append(remote(self.ref.at[tuple(index)], land.at[k - 1], device(**{ax: to})))

        def advance(self):
            if self.going:
                self.finish()
            if self.step < len(self.order):
                self.start()

        def finish(self):
            emit = self.emit if self.step == len(self.order) - 1 else None
            ax = self.order[self.step]
            p = self.dims.index(ax)
            arrived(self.copies)
            land = getattr(r, f"r{self.name}_{self.step}")
            cols = slice(self.lo, self.lo + self.width)
            left = [size[d] for d in self.dims if d != ax]
            total = 1
            for extent in left:
                total *= extent
            into = None if emit else getattr(r, f"s{self.name}_{self.step}")

            def one(flat):
                index, rest_of = [], flat
                for extent in reversed(left):
                    index.insert(0, rest_of % extent if isinstance(rest_of, int) else lax.rem(rest_of, extent))
                    rest_of = rest_of // extent
                full = list(index)
                full.insert(p, at[ax])
                value = self.ref[tuple(full) + (slice(None), cols)].astype(F32)
                for k in range(size[ax] - 1):
                    value += land[(k,) + tuple(index)].astype(F32)
                if emit:
                    emit(index, value)
                else:
                    into[tuple(index)] = value.astype(BF)

            if total <= 2:
                for flat in range(total):
                    one(flat)
            else:
                def body(flat, carry):
                    one(flat)
                    return carry

                lax.fori_loop(0, total, body, 0)
            self.dims.remove(ax)
            self.ref, self.lo, self.step = into, 0, self.step + 1

    def to_rows(out_ref, height, width, lo):
        def emit(index, value):
            step = width // 128
            for j in range(value.shape[1] // 128):
                out_ref[pl.ds(lo // 128 + j, height, stride=step), :] = value[:, j * 128 : j * 128 + 128]

        return emit

    shards = {}

    def to_core(name):
        def emit(index, value):
            shards[name, index[0]] = value
            if index[0] == 1:
                at_lo = slice(PIECE[name][2], PIECE[name][2] + 256)
                halves_of = (shards[name, 0], shards[name, 1])
                r.final[core, :, at_lo] = jnp.where(first_core, *halves_of)
                r.fsend[:, at_lo] = jnp.where(first_core, *reversed(halves_of))

        return emit

    outs = dict(go=(oo_ref, 16, 512), gu=(ou_ref, 16, FF), gd=(od_ref, 64, 512))
    for name, (buf, order, lo, width, height) in enumerate(PIECE):
        emit = to_core(name) if buf == "gq" else to_rows(*outs[buf], lo)
        sums.append(Sum(name, buf, order, width, height, lo, emit))

    load["dy"].wait()
    dy = dyv[...].reshape(256, 512)
    blocks = [(j // 2, j % 2) if na == 2 else (0, j // 2, j % 2) for j in range(4)]
    for j in range(4):
        point()
        cols = slice(j * 512, j * 512 + 512)
        pre = nn(r.n2[...], agu[..., cols].reshape(512, 512))
        sig = 1.0 / (1.0 + jnp.exp(-pre))
        hidden = (pre * sig).astype(BF)
        r.hidden[:, cols] = hidden
        r.dsilu[:, cols] = sig * (1.0 + pre * (1.0 - sig))
        r.gd[blocks[j]] = tn(hidden, dy).astype(BF).reshape(lead[len(blocks[j]) :] + (64, 512))
    for j in range(4):
        point()
        cols = slice(j * 512, j * 512 + 512)
        d_pre = (nt(dy, agd[blocks[j]].reshape(512, 512)) * r.dsilu[:, cols]).astype(BF)
        part = nt(d_pre, agu[..., cols].reshape(512, 512))
        r.dn2[...] = part if j == 0 else r.dn2[...] + part
        r.gu[..., cols] = nn(r.n2t[...], d_pre).astype(BF).reshape(lead + (16, 512))
    point()

    dn2 = r.dn2[...]
    unit = r.unit2[...]
    gains2 = jnp.sum(dn2 * unit, axis=0, keepdims=True)
    d_res = dy.astype(F32) + norm_back(
        dn2 * gf_ref[...], unit, r.inv2[:, 0:1]
    )
    r.dres[...] = d_res
    d_attn = d_res.astype(BF)
    d_mixed = nt(d_attn, w_out).astype(BF)
    for b in range(SEQB):
        for p in range(2):
            part = [d_mixed[b * TOK : (b + 1) * TOK, h * 256 + p * 128 : h * 256 + p * 128 + 128] for h in range(2)]
            r.do[b * 2 + p, core] = jnp.where(first_core, part[0], part[1])
            r.senddo[b * 2 + p] = jnp.where(first_core, part[1], part[0])
    point()
    swap_d = remote(r.senddo, r.do.at[:, core], mate)
    point()
    swap_d.wait_recv()

    def mix_back(n, carry):
        b = n // 2
        q, v, whi = r.q[n], r.v[n], r.whi[n]
        mask, use = r.mask[b], r.use[b]
        share, tot, score = r.share[n], r.tot[n], r.score[n]
        d_out = r.do[n].reshape(256, 128)
        ds = use * nt(d_out, carried(n, 2))
        for m in hm:
            ds += nn((nt(d_out * m, v) * mask).astype(BF), whi * m)
        floor = jnp.maximum(tot, 1.0)
        inv_floor = 1.0 / floor
        prob = share * floor
        dprob = ds * inv_floor
        dscore = prob * (dprob - both(jnp.sum, dprob * prob))
        dnum = dscore * inv_floor * 0.125
        gate = jnp.where(tot > 1.0, 1.0, jnp.where(tot == 1.0, 0.5, 0.0))
        dtot = -(ds * share + dscore * score) * inv_floor * gate
        r.dnum[n] = dnum.astype(BF)
        r.dtot[n] = dtot
        put_state(r.dloc, n, 0, fold(tn((use * dnum).astype(BF), q)))
        put_state(r.dloc, n, 1, fold(tn((use * share).astype(BF), d_out)))
        r.gz[pl.ds(n, 1), :] = jnp.sum(use * dtot, axis=0, keepdims=True)
        return carry

    point()
    lax.fori_loop(0, 4, mix_back, 0)
    point()
    r.gz[4:8, :] = jnp.zeros((4, 128), F32)
    gz_parts = jnp.concatenate(halves(r.gz[...]), axis=0)
    mark = len(started)
    out_3 = spread(r.dloc, r.drcv, gz_parts)

    def mix_back_local(n, carry):
        b = n // 2
        q, k, v, whi, w = r.q[n], r.k[n], r.v[n], r.whi[n], r.w[n]
        mask, maskt, use = r.mask[b], r.maskt[b], r.use[b]
        d_out, dnum = r.do[n].reshape(256, 128), r.dnum[n]
        sb = r.share[n].astype(BF)
        dq = use * nn(dnum, carried(n, 0))
        dk = jnp.zeros((256, 128), F32)
        dv = jnp.zeros((256, 128), F32)
        dw = nn(maskt.astype(BF), r.dtot[n].astype(BF))
        for m in hm:
            dq += nn((nt(dnum * m, whi) * mask).astype(BF), k * m)
            dk += nn((nt(whi * m, dnum) * maskt).astype(BF), q * m)
            dv += nn((nt(whi * m, sb) * maskt).astype(BF), d_out * m)
            dw += nn((nt(v * m, d_out) * maskt).astype(BF), sb * m)
            dw += nn((nt(k * m, q) * maskt).astype(BF), dnum * m)
        cols = pl.ds(pl.multiple_of(lax.rem(n, 2) * 128, 128), 128)
        r.dd[b, :, :, cols] = dq.astype(BF).reshape(2, TOK, 128)
        r.dkl[n] = dk
        r.dvl[n] = dv
        r.dwl[n] = dw
        return carry

    point()
    lax.fori_loop(0, 4, mix_back_local, 0)
    dd = r.dd

    def weight_gradient(lo, width):
        value = nn(r.norm1t[...], dd[:, :, :, lo : lo + width].reshape(512, width))
        r.gq[..., lo : lo + width] = value.astype(BF).reshape(lead + (16, width))

    point()

    arrived(out_3)
    point()
    drcv = r.drcv
    run = jnp.zeros((rows, 128), F32)
    for p in reversed(range(nch)):
        r.dsnd[p] = run.astype(BF)
        here = drcv[p, 0:rows, :].astype(F32)
        if p == nch - 1:
            run = here
        else:
            run = here + (first_of(p, owned) == first_of(p + 1, owned)).astype(F32) * run
    point()
    out_4 = back(r.dsnd, r.gin)
    point()
    zrun = [jnp.zeros((2, 128), F32) for _ in range(SEQB)]
    for p in reversed(range(1, nch)):
        for b in range(SEQB):
            tail = drcv[p, rows : rows + 16, :].astype(F32)
            z = tail[2 * b : 2 * b + 2] + tail[8 + 2 * b : 10 + 2 * b]
            if p < nch - 1:
                z = z + (first_of(p, b) == first_of(p + 1, b)).astype(F32) * zrun[b]
            zrun[b] = jnp.where(p > chip, z, zrun[b])
    after = jnp.minimum(chip + 1, nch - 1)
    for b in range(SEQB):
        r.gz[2 * b : 2 * b + 2, :] = zrun[b]
        matched = (first_of(after, b) == r.info[4 + b : 5 + b, :]) & (chip < nch - 1)
        r.last[b] = r.last[b] * matched.astype(F32)
    point()
    r.go[...] = tn(r.mixed[...], d_attn).astype(BF).reshape(lead + (16, 512))
    point()
    y_rows = r.res[...] + nn(r.hidden[...], agd[...].reshape(FF, 512))
    y_ref[...] = y_rows.astype(BF).reshape(SEQB, TOK, 512)

    point()
    weight_gradient(0, 256)
    point()
    drain(mark)
    arrived(out_4)

    def mix_last(slot, value):
        def one(n, carry):
            cols = pl.ds(pl.multiple_of(slot * 256 + lax.rem(n, 2) * 128, 128), 128)
            dd[n // 2, :, :, cols] = value(n, r.last[n // 2]).astype(BF).reshape(2, TOK, 128)
            return carry

        point()
        lax.fori_loop(0, 4, one, 0)
        point()
        weight_gradient(slot * 256, 256)

    def state_gradient(n, which):
        return get_block(r.gin, n, which).astype(BF)

    def weight_value(n, last):
        more = nt(r.k[n], state_gradient(n, 0)) + nt(r.v[n], state_gradient(n, 1)) + r.gz[pl.ds(n, 1), :]
        return (r.dwl[n] + last * more) * r.w[n]

    mix_last(2, lambda n, last: r.dvl[n] + last * nn(r.whi[n], state_gradient(n, 1)))
    mix_last(1, lambda n, last: r.dkl[n] + last * nn(r.whi[n], state_gradient(n, 0)))
    mix_last(3, weight_value)

    point()
    full_q = agq[...].reshape(512, 1024)
    gains1 = jnp.zeros((1, 512), F32)
    for b in range(SEQB):
        part = nt(dd[b].reshape(256, 1024), full_q)
        r.dn1[:, b] = part.reshape(2, TOK, 512)
        gains1 += jnp.sum(part * r.unit1[b].reshape(256, 512), axis=0, keepdims=True)
    point()
    swap_g = remote(r.dn1.at[1 - core], r.dn1r, mate)

    gains = jnp.concatenate(
        [g[:, j * 128 : j * 128 + 128] for g in (gains1, gains2) for j in range(4)], axis=0
    )

    def exchange(buf, value, me, count, dev):
        buf[me] = value
        return [remote(buf.at[me], buf.at[me], dev(lax.rem(me + k, count))) for k in range(1, count)]

    def total(buf, copies, count):
        arrived(copies)
        value = buf[0]
        for k in range(1, count):
            value = value + buf[k]
        return value

    point()
    copies = exchange(r.gain1, gains, core, 2, lambda t: device(c=t))

    point()
    swap_g.wait_recv()
    point()
    dn1 = (r.dn1[core] + r.dn1r[...]).reshape(256, 512)
    unit = r.unit1[:, core].reshape(256, 512)
    dx = r.dres[...] + norm_back(dn1 * ga_ref[...], unit, r.inv1[:, core].reshape(256, 128)[:, 0:1])
    dx_ref[...] = dx.astype(BF).reshape(SEQB, TOK, 512)

    point()
    gains = total(r.gain1, copies, 2)
    point()
    mark = len(started)
    copies = exchange(r.gain2, gains, chip, nch, chip_device)
    point()
    gains = total(r.gain2, copies, nch)
    point()
    copies = exchange(r.gain3, gains, at["a"], na, lambda t: device(a=t))

    final = r.final
    point()
    swap_f = remote(r.fsend, final.at[core], mate)
    point()
    gains = total(r.gain3, copies, na)
    for ref, first in ((og1_ref, 0), (og2_ref, 4)):
        for j in range(4):
            ref[:, j * 128 : j * 128 + 128] = gains[first + j : first + j + 1]
    point()
    drain(mark)
    swap_f.wait_recv()
    for ref, lo in ((oq_ref, 0), (ok_ref, 256), (ov_ref, 512), (oc_ref, 768)):
        for j in range(4):
            ref[pl.ds(j, 16, stride=4), :] = final[j // 2, :, lo + (j % 2) * 128 : lo + (j % 2) * 128 + 128]
    point()
    drain(len(started))


def hand_over(count, *refs):
    src, dst, held, sems = refs[:count], refs[count : 2 * count], refs[2 * count : 3 * count], refs[3 * count]
    into = [pltpu.make_async_copy(src[n], held[n], sems.at[0, n]) for n in range(count)]
    away = [pltpu.make_async_copy(held[n], dst[n], sems.at[1, n]) for n in range(count)]
    for copy in into:
        copy.start()
    for n in range(count):
        into[n].wait()
        away[n].start()
    for copy in away:
        copy.wait()


def solution(mesh):
    ndp, nseq = mesh.shape["dp"], mesh.shape["seq"]
    joint = D // (ndp * nseq) >= 16
    na = ndp if joint else 1
    ni = nseq // (2 * OUTER)
    scratch = layout(na, ni)
    names = tuple(scratch)
    both_axes = ("dp", "seq")

    def body(x, dy, seg, pad, *args):
        weights, (gain_attn, gain_ffn) = args[:7], args[7:]
        shards = []
        for w in weights:
            if not joint:
                whole = lax.all_gather(w, both_axes, axis=0, tiled=True).reshape(nseq, -1)
                w = lax.dynamic_index_in_dim(whole, lax.axis_index("seq"), 0, keepdims=False)
            shards.append(w.reshape(-1, 128))
        outs = [jax.ShapeDtypeStruct(x.shape, BF)] * 2
        outs += [jax.ShapeDtypeStruct(w.shape, F32) for w in shards]
        outs += [jax.ShapeDtypeStruct((1, D), F32)] * 2
        vmem, hbm = pl.BlockSpec(memory_space=pltpu.VMEM), pl.BlockSpec(memory_space=pltpu.HBM)
        got = pl.pallas_call(
            functools.partial(kernel, na, ni, names),
            out_shape=outs,
            in_specs=[hbm] * 2 + [vmem] * 2 + [hbm] * 7 + [vmem] * 2,
            out_specs=[vmem] * 11,
            scratch_shapes=list(scratch.values()),
            compiler_params=pltpu.CompilerParams(
                collective_id=0, has_side_effects=True, vmem_limit_bytes=62 * 2**20
            ),
            cost_estimate=pl.CostEstimate(flops=12 * 10**9, bytes_accessed=4 * 2**20, transcendentals=10**6),
            name="block",
        )(x, dy, seg, pad, *shards, gain_attn.reshape(1, D), gain_ffn.reshape(1, D))
        got = pl.pallas_call(
            functools.partial(hand_over, 11),
            out_shape=outs,
            in_specs=[hbm] * 11,
            out_specs=[hbm] * 11,
            scratch_shapes=[pltpu.VMEM(o.shape, o.dtype) for o in outs] + [pltpu.SemaphoreType.DMA((2, 11))],
            name="results",
        )(*got)
        y, dx = got[:2]
        grads = [g.reshape(-1) for g in got[2:9]]
        gains = [g.reshape(-1) for g in got[9:]]
        if not joint:
            index = lax.axis_index("dp") * nseq + lax.axis_index("seq")
            grads = [lax.psum(g, "dp") for g in grads]
            grads = [lax.all_gather(g, "seq", axis=0, tiled=True) for g in grads]
            grads = [
                lax.dynamic_slice_in_dim(g, index * (g.shape[0] // (ndp * nseq)), g.shape[0] // (ndp * nseq))
                for g in grads
            ]
            gains = [lax.psum(g, "dp") for g in gains]
        return (y, dx, *grads, *gains)

    data, ids, flat = P("dp", "seq", None), P("dp", "seq"), P(("dp", "seq"))
    return jax.shard_map(
        body,
        mesh=mesh,
        in_specs=(data, data, ids, ids) + (flat,) * 7 + (P(), P()),
        out_specs=(data, data) + (flat,) * 7 + (P(), P()),
        check_vma=False,
    )
```
